32 devices in a mesh: seq: 8 (over y, x, core), chan: 4 (over z).
Axes of the slice: x: 2, y: 2, z: 4, core: 2. Of those that a mesh axis runs over, the one named last changes fastest.
Arguments:
- tokens: bfloat16 [768, 16384], P('chan', 'seq'), may hold values from -7.5 to 7.5
- filter_spectrum: float32 [2, 768, 16384], P(None, 'chan', 'seq'), may hold values from -6 to 6
- skip_weight: float32 [768], P('chan'), may hold values from -1 to 1
- norm_gain: float32 [768], P('chan'), may hold values from 0.5 to 1.5
- mlp_gain: float32 [768], P('chan'), may hold values from 0.5 to 1.5
- mix_in: bfloat16 [4, 36864], P('chan'), may hold values from -0.4375 to 0.4375
- up_weight: bfloat16 [4, 147456], P('chan'), may hold values from -0.4375 to 0.4375
- down_weight: bfloat16 [4, 147456], P('chan'), may hold values from -0.21875 to 0.21875
- mix_out: bfloat16 [4, 36864], P('chan'), may hold values from -0.4375 to 0.4375
Outputs:
- mixed: bfloat16 [768, 16384], P('chan', 'seq')
The draws below stay inside these ranges and needn't reach their ends.
All inputs are finite; a program needn't handle non-finite values.
Results may differ from the reference program's by a relative error of at most 0.013.
Values may be sent and summed in bfloat16 or wider, within the bound.
A program may use at most 64 MiB of HBM per device.

```python
import math
import jax
import jax.numpy as jnp
from jax import lax

D = 768
FF = 3072
BLOCKS = 4
RADIX = 64
TOK_DEV = 2048
TOKENS = 16384
N_SEQ = 8


def draw_tokens(key, part):
    noise_key, col_key = jax.random.split(key)
    channel = jnp.arange(D, dtype=jnp.float32) / D
    scales = 0.1 * 10.0 ** channel
    col_scale = 0.25 * 10.0 ** jax.random.uniform(col_key, (1, TOKENS), jnp.float32)
    values = jax.random.truncated_normal(noise_key, -3.0, 3.0, (D, TOKENS), jnp.float32)
    return (values * scales[:, None] * col_scale).astype(jnp.bfloat16)


def level_of(own_key, shape, pieces, low, largest):
    gain = 1.0
    for dim, blocks in pieces:
        heights = jax.random.uniform(jax.random.fold_in(jax.random.fold_in(own_key, 6), dim), (blocks,), jnp.float32, low / len(pieces), largest / len(pieces))
        gain = gain * jnp.repeat(jnp.exp(heights), shape[dim] // blocks).reshape((-1,) + (1,) * (len(shape) - 1 - dim))
    return gain


def centred(own_key, shape, spread, most, cuts=(), held_as=jnp.bfloat16):
    array = spread * jax.random.normal(own_key, shape, jnp.float32)
    if cuts:
        array = array * level_of(own_key, shape, cuts, -0.22, 0.18)
    return jnp.clip(array, -most, most).astype(held_as)


def setup_inputs(seed: int = 0) -> dict:
    streams_of = jax.random.split(jax.random.key(seed), 10)
    return {
        "tokens": draw_tokens(jax.random.fold_in(streams_of[9], 71), 0),
        "filter_spectrum": centred(streams_of[1], (2, D, TOKENS), 1.0, 6.0, ((1, 4), (2, 8)), jnp.float32),
        "skip_weight": jnp.clip(jax.random.uniform(streams_of[2], (D,), jnp.float32, -1.0, 1.0) * level_of(streams_of[2], (D,), ((0, 4),), -0.4, 0.0), -1.0, 1.0),
        "norm_gain": jnp.clip(1.0 + 0.1 * jax.random.normal(streams_of[3], (D,), jnp.float32), 0.5, 1.5),
        "mlp_gain": jnp.clip(1.0 + 0.1 * jax.random.normal(streams_of[4], (D,), jnp.float32), 0.5, 1.5),
        "mix_in": centred(streams_of[5], (BLOCKS, (D // BLOCKS) * (D // BLOCKS)), (D // BLOCKS) ** -0.5, 0.4375, ((0, 4),)),
        "up_weight": centred(streams_of[6], (BLOCKS, (D // BLOCKS) * (FF // BLOCKS)), (D // BLOCKS) ** -0.5, 0.4375, ((0, 4),)),
        "down_weight": centred(streams_of[7], (BLOCKS, (FF // BLOCKS) * (D // BLOCKS)), (FF // BLOCKS) ** -0.5, 0.21875, ((0, 4),)),
        "mix_out": centred(streams_of[8], (BLOCKS, (D // BLOCKS) * (D // BLOCKS)), (D // BLOCKS) ** -0.5, 0.4375, ((0, 4),)),
    }


def dft_tables(length_dft):
    position = jnp.arange(length_dft, dtype=jnp.int32)
    phase_int = position[:, None] * position[None, :] % length_dft
    radians = phase_int.astype(jnp.float32) * (2.0 * math.pi / length_dft)
    return (jnp.cos(radians).astype(jnp.bfloat16), jnp.sin(radians).astype(jnp.bfloat16))

def twiddle_tables(wide, narrow):
    outer_idx = jnp.arange(wide, dtype=jnp.int32)
    inner_idx = jnp.arange(narrow, dtype=jnp.int32)
    phase_int = outer_idx[:, None] * inner_idx[None, :] % (wide * narrow)
    radians = phase_int.astype(jnp.float32) * (2.0 * math.pi / (wide * narrow))
    return (jnp.cos(radians)[None], jnp.sin(radians)[None])

def mix_form(form, left_op, right_op):
    return jnp.einsum(form, left_op.astype(jnp.float32), right_op.astype(jnp.float32))

def forward_local(values, tables):
    cos_w, sin_w, cos_a, sin_a = tables
    rows_all, length_dft = values.shape
    wide = cos_w.shape[0]
    narrow = length_dft // wide
    grid = values.reshape(rows_all, wide, narrow)
    section_re = mix_form('rba,bk->rka', grid, cos_w)
    section_im = -mix_form('rba,bk->rka', grid, sin_w)
    twid_cos, twid_sin = twiddle_tables(wide, narrow)
    inner_re = (section_re * twid_cos + section_im * twid_sin).astype(jnp.bfloat16)
    inner_im = (section_im * twid_cos - section_re * twid_sin).astype(jnp.bfloat16)
    out_re = mix_form('rka,ad->rdk', inner_re, cos_a) + mix_form('rka,ad->rdk', inner_im, sin_a)
    out_im = mix_form('rka,ad->rdk', inner_im, cos_a) - mix_form('rka,ad->rdk', inner_re, sin_a)
    return (out_re.reshape(rows_all, length_dft), out_im.reshape(rows_all, length_dft))

def inverse_local(values_re, values_im, tables):
    cos_w, sin_w, cos_a, sin_a = tables
    rows_all, length_dft = values_re.shape
    wide = cos_w.shape[0]
    narrow = length_dft // wide
    grid_re = values_re.reshape(rows_all, narrow, wide)
    grid_im = values_im.reshape(rows_all, narrow, wide)
    back_re = mix_form('rdk,da->rka', grid_re, cos_a) - mix_form('rdk,da->rka', grid_im, sin_a)
    back_im = mix_form('rdk,da->rka', grid_im, cos_a) + mix_form('rdk,da->rka', grid_re, sin_a)
    twid_cos, twid_sin = twiddle_tables(wide, narrow)
    outer_re = (back_re * twid_cos - back_im * twid_sin).astype(jnp.bfloat16)
    outer_im = (back_im * twid_cos + back_re * twid_sin).astype(jnp.bfloat16)
    real_part = mix_form('rka,kb->rba', outer_re, cos_w) - mix_form('rka,kb->rba', outer_im, sin_w)
    return real_part.reshape(rows_all, length_dft)

def product_first(left_op, right_op):
    return jnp.dot(left_op.T, right_op, preferred_element_type=jnp.float32)

def normalize(values, gain_col):
    mean_val = lax.optimization_barrier(jnp.sum(values, axis=0, keepdims=True)) / D
    square = lax.optimization_barrier(jnp.sum(values * values, axis=0, keepdims=True)) / D
    return (values - mean_val) * lax.rsqrt(square - mean_val * mean_val + 1e-05) * gain_col[:, None]

def convolve(normed, spectrum, tables, cos_p, sin_p):
    col_width = normed.shape[0]
    share = TOK_DEV // N_SEQ
    grid = normed.reshape(col_width * N_SEQ, TOK_DEV)
    first_re, first_im = forward_local(grid, tables)
    first_re = first_re.reshape(col_width, N_SEQ, TOK_DEV)
    first_im = first_im.reshape(col_width, N_SEQ, TOK_DEV)
    frequency = jnp.arange(TOK_DEV, dtype=jnp.int32)
    devices = jnp.arange(N_SEQ, dtype=jnp.int32)
    radians = (devices[:, None] * frequency[None, :]).astype(jnp.float32) * (2.0 * math.pi / TOKENS)
    twist_cos = jnp.cos(radians)[None]
    twist_sin = jnp.sin(radians)[None]
    twisted_re = (first_re * twist_cos + first_im * twist_sin).astype(jnp.bfloat16)
    twisted_im = (first_im * twist_cos - first_re * twist_sin).astype(jnp.bfloat16)
    tw_re = twisted_re.astype(jnp.float32).reshape(col_width, N_SEQ, N_SEQ, share)
    tw_im = twisted_im.astype(jnp.float32).reshape(col_width, N_SEQ, N_SEQ, share)
    cp = cos_p.astype(jnp.float32)
    sp = sin_p.astype(jnp.float32)
    spec_re = jnp.einsum('gp,cpqr->cqgr', cp, tw_re) + jnp.einsum('gp,cpqr->cqgr', sp, tw_im)
    spec_im = jnp.einsum('gp,cpqr->cqgr', cp, tw_im) - jnp.einsum('gp,cpqr->cqgr', sp, tw_re)
    filter_re = spectrum[0].reshape(col_width, N_SEQ, N_SEQ, share)
    filter_im = spectrum[1].reshape(col_width, N_SEQ, N_SEQ, share)
    filtered_re = (filter_re * spec_re - filter_im * spec_im).astype(jnp.bfloat16).astype(jnp.float32)
    filtered_im = (filter_re * spec_im + filter_im * spec_re).astype(jnp.bfloat16).astype(jnp.float32)
    back_re = jnp.einsum('pg,cqgr->cqpr', cp, filtered_re) - jnp.einsum('pg,cqgr->cqpr', sp, filtered_im)
    back_im = jnp.einsum('pg,cqgr->cqpr', cp, filtered_im) + jnp.einsum('pg,cqgr->cqpr', sp, filtered_re)
    owned = devices[:, None] * share + jnp.arange(share, dtype=jnp.int32)[None, :]
    undo = (devices[None, :, None] * owned[:, None, :]).astype(jnp.float32) * (2.0 * math.pi / TOKENS)
    undo_cos = jnp.cos(undo)[None]
    undo_sin = jnp.sin(undo)[None]
    turned_re = (back_re * undo_cos - back_im * undo_sin).astype(jnp.bfloat16)
    turned_im = (back_im * undo_cos + back_re * undo_sin).astype(jnp.bfloat16)
    home_re = jnp.transpose(turned_re, (0, 2, 1, 3)).reshape(col_width * N_SEQ, TOK_DEV)
    home_im = jnp.transpose(turned_im, (0, 2, 1, 3)).reshape(col_width * N_SEQ, TOK_DEV)
    result = inverse_local(home_re, home_im, tables) * (1.0 / TOKENS)
    return result.reshape(col_width, TOKENS)

def reference(tokens, filter_spectrum, skip_weight, norm_gain, mlp_gain, mix_in, up_weight, down_weight, mix_out):
    inputs = tokens.astype(jnp.float32)
    normed = normalize(inputs, norm_gain).astype(jnp.bfloat16)
    cos_w, sin_w = dft_tables(RADIX)
    cos_a, sin_a = dft_tables(TOK_DEV // RADIX)
    tables = (cos_w, sin_w, cos_a, sin_a)
    cos_p, sin_p = dft_tables(N_SEQ)
    part_width = D // BLOCKS
    piece_width = part_width // BLOCKS
    hidden_width = FF // BLOCKS
    columns = []
    for block_id in range(BLOCKS):
        low_row = block_id * part_width
        columns.append(convolve(normed[low_row:low_row + part_width], filter_spectrum[:, low_row:low_row + part_width], tables, cos_p, sin_p))
    convolved = jnp.concatenate(columns, axis=0)
    residual = (inputs + convolved + skip_weight[:, None] * normed.astype(jnp.float32)).astype(jnp.bfloat16)
    second = normalize(residual.astype(jnp.float32), mlp_gain).astype(jnp.bfloat16)
    firsts = []
    for block_id in range(BLOCKS):
        low_row = block_id * part_width
        weight_block = mix_in[block_id].reshape(part_width, part_width)
        firsts.append(product_first(weight_block, second[low_row:low_row + part_width]).astype(jnp.bfloat16))
    stacked = jnp.stack(firsts, axis=0).reshape(BLOCKS, BLOCKS, piece_width, TOKENS)
    regrouped = jnp.swapaxes(stacked, 0, 1).reshape(BLOCKS, part_width, TOKENS)
    lowered = []
    for block_id in range(BLOCKS):
        up_block = up_weight[block_id].reshape(part_width, hidden_width)
        down_block = down_weight[block_id].reshape(hidden_width, part_width)
        hidden = jax.nn.gelu(product_first(up_block, regrouped[block_id]), approximate=False).astype(jnp.bfloat16)
        lowered.append(product_first(down_block, hidden).astype(jnp.bfloat16))
    lowered = jnp.stack(lowered, axis=0).reshape(BLOCKS, BLOCKS, piece_width, TOKENS)
    returned = jnp.swapaxes(lowered, 0, 1).reshape(BLOCKS, part_width, TOKENS)
    outputs = []
    for block_id in range(BLOCKS):
        outputs.append(product_first(mix_out[block_id].reshape(part_width, part_width), returned[block_id]))
    return (residual.astype(jnp.float32) + jnp.concatenate(outputs, axis=0)).astype(jnp.bfloat16)
```

```python
import functools
import math

import jax
import jax.numpy as jnp
import numpy as np
from jax import lax
from jax.experimental import pallas as pl
from jax.experimental.pallas import tpu as pltpu
from jax.sharding import PartitionSpec as P

RADIX = 64


def dft_tables(length_dft):
    position = jnp.arange(length_dft, dtype=jnp.int32)
    phase_int = position[:, None] * position[None, :] % length_dft
    radians = phase_int.astype(jnp.float32) * (2.0 * math.pi / length_dft)
    return (jnp.cos(radians).astype(jnp.bfloat16), jnp.sin(radians).astype(jnp.bfloat16))


def twiddle_tables(wide, narrow):
    outer_idx = jnp.arange(wide, dtype=jnp.int32)
    inner_idx = jnp.arange(narrow, dtype=jnp.int32)
    phase_int = outer_idx[:, None] * inner_idx[None, :] % (wide * narrow)
    radians = phase_int.astype(jnp.float32) * (2.0 * math.pi / (wide * narrow))
    return (jnp.cos(radians)[None], jnp.sin(radians)[None])


def mix_form(form, left_op, right_op):
    return jnp.einsum(form, left_op.astype(jnp.float32), right_op.astype(jnp.float32))


def forward_local(values, tables):
    cos_w, sin_w, cos_a, sin_a = tables
    rows_all, length_dft = values.shape
    wide = cos_w.shape[0]
    narrow = length_dft // wide
    grid = values.reshape(rows_all, wide, narrow)
    section_re = mix_form("rba,bk->rka", grid, cos_w)
    section_im = -mix_form("rba,bk->rka", grid, sin_w)
    twid_cos, twid_sin = twiddle_tables(wide, narrow)
    inner_re = (section_re * twid_cos + section_im * twid_sin).astype(jnp.bfloat16)
    inner_im = (section_im * twid_cos - section_re * twid_sin).astype(jnp.bfloat16)
    out_re = mix_form("rka,ad->rdk", inner_re, cos_a) + mix_form("rka,ad->rdk", inner_im, sin_a)
    out_im = mix_form("rka,ad->rdk", inner_im, cos_a) - mix_form("rka,ad->rdk", inner_re, sin_a)
    return (out_re.reshape(rows_all, length_dft), out_im.reshape(rows_all, length_dft))


def inverse_local(values_re, values_im, tables):
    cos_w, sin_w, cos_a, sin_a = tables
    rows_all, length_dft = values_re.shape
    wide = cos_w.shape[0]
    narrow = length_dft // wide
    grid_re = values_re.reshape(rows_all, narrow, wide)
    grid_im = values_im.reshape(rows_all, narrow, wide)
    back_re = mix_form("rdk,da->rka", grid_re, cos_a) - mix_form("rdk,da->rka", grid_im, sin_a)
    back_im = mix_form("rdk,da->rka", grid_im, cos_a) + mix_form("rdk,da->rka", grid_re, sin_a)
    twid_cos, twid_sin = twiddle_tables(wide, narrow)
    outer_re = (back_re * twid_cos - back_im * twid_sin).astype(jnp.bfloat16)
    outer_im = (back_im * twid_cos + back_re * twid_sin).astype(jnp.bfloat16)
    real_part = mix_form("rka,kb->rba", outer_re, cos_w) - mix_form("rka,kb->rba", outer_im, sin_w)
    return real_part.reshape(rows_all, length_dft)


def small_mix(table, values):
    return jnp.einsum("gp,cpr->cgr", table.astype(jnp.float32), values.astype(jnp.float32))


def spectral(normed, spectrum, tables, cos_p, sin_p, send_out, send_back):
    col_width, tok_rows = normed.shape
    groups = cos_p.shape[0]
    share = tok_rows // groups
    length_all = tok_rows * groups
    device_pos = lax.axis_index("seq")
    frequency = jnp.arange(tok_rows, dtype=jnp.int32)
    radians = (frequency * device_pos).astype(jnp.float32) * (2.0 * math.pi / length_all)
    twist_cos = jnp.cos(radians)[None, :]
    twist_sin = jnp.sin(radians)[None, :]
    first_re, first_im = forward_local(normed, tables)
    twisted_re = (first_re * twist_cos + first_im * twist_sin).astype(jnp.bfloat16)
    twisted_im = (first_im * twist_cos - first_re * twist_sin).astype(jnp.bfloat16)
    moved_re, moved_im = send_out((twisted_re, twisted_im))
    moved_re = moved_re.reshape(col_width, groups, share)
    moved_im = moved_im.reshape(col_width, groups, share)
    spec_re = small_mix(cos_p, moved_re) + small_mix(sin_p, moved_im)
    spec_im = small_mix(cos_p, moved_im) - small_mix(sin_p, moved_re)
    filter_re = spectrum[0].reshape(col_width, groups, share)
    filter_im = spectrum[1].reshape(col_width, groups, share)
    filtered_re = (filter_re * spec_re - filter_im * spec_im).astype(jnp.bfloat16)
    filtered_im = (filter_re * spec_im + filter_im * spec_re).astype(jnp.bfloat16)
    back_re = small_mix(cos_p, filtered_re) - small_mix(sin_p, filtered_im)
    back_im = small_mix(cos_p, filtered_im) + small_mix(sin_p, filtered_re)
    owned_freq = device_pos * share + jnp.arange(share, dtype=jnp.int32)
    devices = jnp.arange(groups, dtype=jnp.int32)
    undo_radians = (devices[:, None] * owned_freq[None, :]).astype(jnp.float32) * (
        2.0 * math.pi / length_all
    )
    undo_cos = jnp.cos(undo_radians)[None]
    undo_sin = jnp.sin(undo_radians)[None]
    turned_re = (
        (back_re * undo_cos - back_im * undo_sin).astype(jnp.bfloat16).reshape(col_width, tok_rows)
    )
    turned_im = (
        (back_im * undo_cos + back_re * undo_sin).astype(jnp.bfloat16).reshape(col_width, tok_rows)
    )
    home_re, home_im = send_back((turned_re, turned_im))
    return inverse_local(home_re, home_im, tables) * (1.0 / length_all)


MESH = pl.DeviceIdType.MESH
VMEM_BYTES = 56 * 1024 * 1024


def vmem_spec():
    return pl.BlockSpec(memory_space=pltpu.VMEM)


def greet(axis, n):
    me = lax.axis_index(axis)
    barrier = pltpu.get_barrier_semaphore()
    for k in range(1, n):
        pl.semaphore_signal(
            barrier, inc=1, device_id={axis: lax.rem(me + k, n)}, device_id_type=MESH
        )
    return barrier


def share_stats(n, barrier, stats, send_sem, recv_sem):
    me = lax.axis_index("chan")
    pl.semaphore_wait(barrier, n - 1)
    copies = []
    for k in range(1, n):
        copy = pltpu.make_async_remote_copy(
            src_ref=stats.at[0],
            dst_ref=stats.at[k],
            send_sem=send_sem.at[k],
            recv_sem=recv_sem.at[k],
            device_id={"chan": lax.rem(me + k, n)},
            device_id_type=MESH,
        )
        copy.start()
        copies.append(copy)
    for copy in copies:
        copy.wait()
    total = stats[0]
    for k in range(1, n):
        total = total + stats[k]
    return total


def norm_kernel(n, width, x_ref, gain_ref, out_ref, stats, send_sem, recv_sem):
    barrier = greet("chan", n)
    cols = x_ref.shape[1]
    step = min(cols, 512)
    for c in range(0, cols, step):
        x = x_ref[:, c : c + step].astype(jnp.float32)
        stats[0, 0:1, c : c + step] = jnp.sum(x, axis=0, keepdims=True)
        stats[0, 1:2, c : c + step] = jnp.sum(x * x, axis=0, keepdims=True)
    total = share_stats(n, barrier, stats, send_sem, recv_sem)
    mean = total[0:1] / width
    scale = lax.rsqrt(total[1:2] / width - mean * mean + 1e-05)
    gain = gain_ref[...]
    for c in range(0, cols, step):
        x = x_ref[:, c : c + step].astype(jnp.float32)
        y = (x - mean[:, c : c + step]) * scale[:, c : c + step] * gain
        out_ref[:, c : c + step] = y.astype(jnp.bfloat16)


def first_norm(n, width, tokens, gain):
    return pl.pallas_call(
        functools.partial(norm_kernel, n, width),
        out_shape=jax.ShapeDtypeStruct(tokens.shape, jnp.bfloat16),
        in_specs=[vmem_spec()] * 2,
        out_specs=vmem_spec(),
        scratch_shapes=[
            pltpu.VMEM((n, 2, tokens.shape[1]), jnp.float32),
            pltpu.SemaphoreType.DMA((n,)),
            pltpu.SemaphoreType.DMA((n,)),
        ],
        compiler_params=pltpu.CompilerParams(
            collective_id=0, has_side_effects=True, vmem_limit_bytes=VMEM_BYTES
        ),
    )(tokens, gain[:, None])


def small_dft(values, sign):
    n = len(values)
    if n == 1:
        return values
    even = small_dft(values[0::2], sign)
    odd = small_dft(values[1::2], sign)
    out = [None] * n
    for k in range(n // 2):
        re, im = odd[k]
        if k == 0:
            tr, ti = re, im
        elif 4 * k == n:
            tr, ti = (-im, re) if sign > 0 else (im, -re)
        else:
            c = float(np.float64(math.cos(2 * math.pi * k / n)).astype(jnp.bfloat16))
            s = sign * float(np.float64(math.sin(2 * math.pi * k / n)).astype(jnp.bfloat16))
            tr, ti = re * c - im * s, re * s + im * c
        er, ei = even[k]
        out[k] = (er + tr, ei + ti)
        out[k + n // 2] = (er - tr, ei - ti)
    return out


def conv_kernel(
    n, x_ref, filt_hbm, cos_hbm, sin_hbm, twc_ref, tws_ref, undo_c, undo_s, out_ref,
    cos_v, sin_v, filt_v, send_f, recv_f, send_b, recv_b,
    load_sem, filt_sem, sf_sem, rf_sem, sb_sem, rb_sem,
):
    me = lax.axis_index("seq")
    barrier = greet("seq", n)
    rows, cols = x_ref.shape
    share = cols // n
    parts = sb_sem.shape[1]
    group = rows // parts

    def block_of(k):
        return pl.ds(pl.multiple_of(lax.rem(me + k, n) * share, share), share)

    def load(k, which):
        hbm, vmem = ((cos_hbm, cos_v), (sin_hbm, sin_v))[which]
        view = block_of(k)
        return pltpu.make_async_copy(hbm.at[:, view], vmem.at[:, view], load_sem.at[k, which])

    filt_copy = pltpu.make_async_copy(filt_hbm, filt_v, filt_sem.at[0])
    for k in list(range(1, n)) + [0]:
        load(k, 0).start()
        load(k, 1).start()
    filt_copy.start()
    pl.semaphore_wait(barrier, n - 1)

    def transform(k):
        load(k, 0).wait()
        load(k, 1).wait()
        view = block_of(k)
        x = x_ref[...]
        re = jnp.dot(x, cos_v[:, view], preferred_element_type=jnp.float32)
        im = -jnp.dot(x, sin_v[:, view], preferred_element_type=jnp.float32)
        tc, ts = twc_ref[:, view], tws_ref[:, view]
        return (
            (re * tc + im * ts).astype(jnp.bfloat16),
            (im * tc - re * ts).astype(jnp.bfloat16),
        )

    def outward(k):
        peer = lax.rem(me + k, n)
        return pltpu.make_async_remote_copy(
            src_ref=send_f.at[k],
            dst_ref=recv_f.at[me],
            send_sem=sf_sem.at[k],
            recv_sem=rf_sem.at[k],
            device_id={"seq": peer},
            device_id_type=MESH,
        )

    def forward(k, carry):
        re, im = transform(k)
        send_f[k, 0] = re
        send_f[k, 1] = im
        outward(k).start()
        return carry

    lax.fori_loop(1, n, forward, 0)
    re, im = transform(0)
    recv_f[me, 0] = re
    recv_f[me, 1] = im
    filt_copy.wait()

    def arrive(k, carry):
        outward(k).wait()
        return carry

    lax.fori_loop(1, n, arrive, 0)

    def inward(k, part):
        peer = lax.rem(me + k, n)
        view = pl.ds(part * group, group)
        return pltpu.make_async_remote_copy(
            src_ref=send_b.at[peer, :, view],
            dst_ref=recv_b.at[k, :, view],
            send_sem=sb_sem.at[k, part],
            recv_sem=rb_sem.at[k, part],
            device_id={"seq": peer},
            device_id_type=MESH,
        )

    lanes = 128
    for part in range(parts):

        def middle(i, carry, part=part):
            view = pl.ds(pl.multiple_of(part * group + i * 16, 16), 16)
            for c in range(0, share, lanes):
                values = [
                    (
                        recv_f[p, 0, view, c : c + lanes].astype(jnp.float32),
                        recv_f[p, 1, view, c : c + lanes].astype(jnp.float32),
                    )
                    for p in range(n)
                ]
                spec = small_dft(values, -1)
                filtered = []
                for g in range(n):
                    sr, si = spec[g]
                    low = g * share + c
                    fr = filt_v[0, view, low : low + lanes]
                    fi = filt_v[1, view, low : low + lanes]
                    filtered.append((fr * sr - fi * si, fr * si + fi * sr))
                back = small_dft(filtered, 1)
                for p in range(n):
                    br, bi = back[p]
                    uc = undo_c[p : p + 1, c : c + lanes]
                    us = undo_s[p : p + 1, c : c + lanes]
                    send_b[p, 0, view, c : c + lanes] = (br * uc - bi * us).astype(jnp.bfloat16)
                    send_b[p, 1, view, c : c + lanes] = (bi * uc + br * us).astype(jnp.bfloat16)
            return carry

        lax.fori_loop(0, group // 16, middle, 0)

        def push(k, carry, part=part):
            inward(k, part).start()
            return carry

        lax.fori_loop(1, n, push, 0)

    tile = min(cols, 512)
    scale = 1.0 / (n * cols)

    def accumulate(re, im, source, first):
        view = pl.ds(pl.multiple_of(source * share, share), share)

        def column(t, carry):
            low = pl.ds(pl.multiple_of(t * tile, tile), tile)
            term = jnp.dot(re, cos_v[view, low], preferred_element_type=jnp.float32) - jnp.dot(
                im, sin_v[view, low], preferred_element_type=jnp.float32
            )
            if first:
                out_ref[:, low] = term * scale
            else:
                out_ref[:, low] += term * scale
            return carry

        lax.fori_loop(0, cols // tile, column, 0)

    accumulate(send_b[me, 0], send_b[me, 1], me, True)

    def back_step(k, carry):
        for part in range(parts):
            inward(k, part).wait()
        accumulate(recv_b[k, 0], recv_b[k, 1], lax.rem(me + n - k, n), False)
        return carry

    lax.fori_loop(1, n, back_step, 0)


def convolve_kernel(n, normed, spectrum):
    rows, cols = normed.shape
    share = cols // n
    index = np.arange(cols)
    angle = (index[:, None] * index[None, :] % cols) * (2.0 * math.pi / cols)
    cos_m = jnp.asarray(np.cos(angle).astype(jnp.bfloat16))
    sin_m = jnp.asarray(np.sin(angle).astype(jnp.bfloat16))
    pos = lax.axis_index("seq")
    turn = 2.0 * math.pi / (n * cols)
    twist = (jnp.arange(cols, dtype=jnp.int32) * pos).astype(jnp.float32)[None] * turn
    owned = pos * share + jnp.arange(share, dtype=jnp.int32)
    undo = (jnp.arange(n, dtype=jnp.int32)[:, None] * owned[None]).astype(jnp.float32) * turn
    parts = 4 if rows % 64 == 0 else 1
    block = pltpu.VMEM((n, 2, rows, share), jnp.bfloat16)
    dma = pltpu.SemaphoreType.DMA
    return pl.pallas_call(
        functools.partial(conv_kernel, n),
        out_shape=jax.ShapeDtypeStruct((rows, cols), jnp.float32),
        in_specs=[vmem_spec()] + [pl.BlockSpec(memory_space=pl.ANY)] * 3 + [vmem_spec()] * 4,
        out_specs=vmem_spec(),
        scratch_shapes=[
            pltpu.VMEM((cols, cols), jnp.bfloat16),
            pltpu.VMEM((cols, cols), jnp.bfloat16),
            pltpu.VMEM(spectrum.shape, jnp.float32),
            block, block, block, block,
            dma((n, 2)), dma((1,)), dma((n,)), dma((n,)), dma((n, parts)), dma((n, parts)),
        ],
        compiler_params=pltpu.CompilerParams(
            collective_id=1, has_side_effects=True, vmem_limit_bytes=VMEM_BYTES
        ),
    )(normed, spectrum, cos_m, sin_m, jnp.cos(twist), jnp.sin(twist), jnp.cos(undo), jnp.sin(undo))


def across(left, right):
    return lax.dot_general(
        left, right, (((0,), (0,)), ((), ())), preferred_element_type=jnp.float32
    )


def mlp_kernel(
    n, width, tok_ref, conv_ref, norm_ref, skip_ref, gain_ref, mi_ref, up_ref, down_ref, mo_ref,
    out_ref, resid, stats, first, regrouped, lowered, returned,
    st_send, st_recv, send_sem, recv_sem,
):
    me = lax.axis_index("chan")
    barrier = greet("chan", n)
    rows, cols = tok_ref.shape
    chunks, _, step = first.shape
    piece = rows // n

    def residual_of(c, carry):
        view = pl.ds(pl.multiple_of(c * step, step), step)
        value = (
            tok_ref[:, view].astype(jnp.float32)
            + conv_ref[:, view]
            + skip_ref[...] * norm_ref[:, view].astype(jnp.float32)
        ).astype(jnp.bfloat16)
        resid[:, view] = value
        value = value.astype(jnp.float32)
        stats[0, 0:1, view] = jnp.sum(value, axis=0, keepdims=True)
        stats[0, 1:2, view] = jnp.sum(value * value, axis=0, keepdims=True)
        return carry

    lax.fori_loop(0, chunks, residual_of, 0)
    total = share_stats(n, barrier, stats, st_send, st_recv)
    mean = total[0:1] / width
    stats[0, 0:1, :] = mean
    stats[0, 1:2, :] = lax.rsqrt(total[1:2] / width - mean * mean + 1e-05)

    def exchange(phase, c, k):
        peer = lax.rem(me + k, n)
        source, target = ((first, regrouped), (lowered, returned))[phase]
        return pltpu.make_async_remote_copy(
            src_ref=source.at[c, pl.ds(pl.multiple_of(peer * piece, 16), piece)],
            dst_ref=target.at[c, pl.ds(pl.multiple_of(me * piece, 16), piece)],
            send_sem=send_sem.at[phase, c, k],
            recv_sem=recv_sem.at[phase, c, k],
            device_id={"chan": peer},
            device_id_type=MESH,
        )

    own = pl.ds(pl.multiple_of(me * piece, 16), piece)

    def first_step(c, carry):
        view = pl.ds(pl.multiple_of(c * step, step), step)
        value = resid[:, view].astype(jnp.float32)
        value = (value - stats[0, 0:1, view]) * stats[0, 1:2, view] * gain_ref[...]
        first[c] = across(mi_ref[...], value.astype(jnp.bfloat16)).astype(jnp.bfloat16)
        for k in range(1, n):
            exchange(0, c, k).start()
        regrouped[c, own] = first[c, own]
        return carry

    lax.fori_loop(0, chunks, first_step, 0)

    def second_step(c, carry):
        for k in range(1, n):
            exchange(0, c, k).wait()
        pre = across(up_ref[...], regrouped[c])
        hidden = 0.5 * pre * (1.0 + lax.erf(pre * math.sqrt(0.5)))
        lowered[c] = across(down_ref[...], hidden.astype(jnp.bfloat16)).astype(jnp.bfloat16)
        for k in range(1, n):
            exchange(1, c, k).start()
        returned[c, own] = lowered[c, own]
        return carry

    lax.fori_loop(0, chunks, second_step, 0)

    def third_step(c, carry):
        view = pl.ds(pl.multiple_of(c * step, step), step)
        for k in range(1, n):
            exchange(1, c, k).wait()
        term = across(mo_ref[...], returned[c])
        out_ref[:, view] = (resid[:, view].astype(jnp.float32) + term).astype(jnp.bfloat16)
        return carry

    lax.fori_loop(0, chunks, third_step, 0)


def mlp(n, width, *operands):
    rows, cols = operands[0].shape
    step = 256 if cols % 256 == 0 else cols
    chunks = cols // step
    block = pltpu.VMEM((chunks, rows, step), jnp.bfloat16)
    dma = pltpu.SemaphoreType.DMA
    return pl.pallas_call(
        functools.partial(mlp_kernel, n, width),
        out_shape=jax.ShapeDtypeStruct((rows, cols), jnp.bfloat16),
        in_specs=[vmem_spec()] * len(operands),
        out_specs=vmem_spec(),
        scratch_shapes=[
            pltpu.VMEM((rows, cols), jnp.bfloat16),
            pltpu.VMEM((n, 2, cols), jnp.float32),
            block, block, block, block,
            dma((n,)), dma((n,)), dma((2, chunks, n)), dma((2, chunks, n)),
        ],
        compiler_params=pltpu.CompilerParams(
            collective_id=2, has_side_effects=True, vmem_limit_bytes=VMEM_BYTES
        ),
    )(*operands)


def shards(
    tokens,
    filter_spectrum,
    skip_weight,
    norm_gain,
    mlp_gain,
    mix_in,
    up_weight,
    down_weight,
    mix_out,
):
    columns, tok_rows = tokens.shape
    groups = lax.axis_size("seq")
    blocks = lax.axis_size("chan")
    width = columns * blocks
    normed = first_norm(blocks, width, tokens, norm_gain)
    if groups == 8 and (tok_rows // groups) % 128 == 0:
        convolved = convolve_kernel(groups, normed, filter_spectrum)
    else:
        cos_w, sin_w = dft_tables(RADIX)
        cos_a, sin_a = dft_tables(tok_rows // RADIX)
        cos_p, sin_p = dft_tables(groups)

        def swap(pair_in):
            return tuple(
                lax.all_to_all(half, "seq", split_axis=1, concat_axis=1, tiled=True)
                for half in pair_in
            )

        convolved = spectral(
            normed, filter_spectrum, (cos_w, sin_w, cos_a, sin_a), cos_p, sin_p, swap, swap
        )
    hidden_width = up_weight.shape[1] // columns
    return mlp(
        blocks,
        width,
        tokens,
        convolved,
        normed,
        skip_weight[:, None],
        mlp_gain[:, None],
        mix_in.reshape(columns, columns),
        up_weight.reshape(columns, hidden_width),
        down_weight.reshape(hidden_width, columns),
        mix_out.reshape(columns, columns),
    )


def solution(mesh):
    in_specs = (
        P("chan", "seq"),
        P(None, "chan", "seq"),
        P("chan"),
        P("chan"),
        P("chan"),
        P("chan", None),
        P("chan", None),
        P("chan", None),
        P("chan", None),
    )
    out_specs = P("chan", "seq")
    return jax.shard_map(shards, mesh=mesh, in_specs=in_specs, out_specs=out_specs, check_vma=False)
```

```python
import functools
import math

import jax
import jax.numpy as jnp
import numpy as np
from jax import lax
from jax.experimental import pallas as pl
from jax.experimental.pallas import tpu as pltpu
from jax.sharding import PartitionSpec as P

RADIX = 64


def dft_tables(length_dft):
    position = jnp.arange(length_dft, dtype=jnp.int32)
    phase_int = position[:, None] * position[None, :] % length_dft
    radians = phase_int.astype(jnp.float32) * (2.0 * math.pi / length_dft)
    return (jnp.cos(radians).astype(jnp.bfloat16), jnp.sin(radians).astype(jnp.bfloat16))


def twiddle_tables(wide, narrow):
    outer_idx = jnp.arange(wide, dtype=jnp.int32)
    inner_idx = jnp.arange(narrow, dtype=jnp.int32)
    phase_int = outer_idx[:, None] * inner_idx[None, :] % (wide * narrow)
    radians = phase_int.astype(jnp.float32) * (2.0 * math.pi / (wide * narrow))
    return (jnp.cos(radians)[None], jnp.sin(radians)[None])


def mix_form(form, left_op, right_op):
    return jnp.einsum(form, left_op.astype(jnp.float32), right_op.astype(jnp.float32))


def forward_local(values, tables):
    cos_w, sin_w, cos_a, sin_a = tables
    rows_all, length_dft = values.shape
    wide = cos_w.shape[0]
    narrow = length_dft // wide
    grid = values.reshape(rows_all, wide, narrow)
    section_re = mix_form("rba,bk->rka", grid, cos_w)
    section_im = -mix_form("rba,bk->rka", grid, sin_w)
    twid_cos, twid_sin = twiddle_tables(wide, narrow)
    inner_re = (section_re * twid_cos + section_im * twid_sin).astype(jnp.bfloat16)
    inner_im = (section_im * twid_cos - section_re * twid_sin).astype(jnp.bfloat16)
    out_re = mix_form("rka,ad->rdk", inner_re, cos_a) + mix_form("rka,ad->rdk", inner_im, sin_a)
    out_im = mix_form("rka,ad->rdk", inner_im, cos_a) - mix_form("rka,ad->rdk", inner_re, sin_a)
    return (out_re.reshape(rows_all, length_dft), out_im.reshape(rows_all, length_dft))


def inverse_local(values_re, values_im, tables):
    cos_w, sin_w, cos_a, sin_a = tables
    rows_all, length_dft = values_re.shape
    wide = cos_w.shape[0]
    narrow = length_dft // wide
    grid_re = values_re.reshape(rows_all, narrow, wide)
    grid_im = values_im.reshape(rows_all, narrow, wide)
    back_re = mix_form("rdk,da->rka", grid_re, cos_a) - mix_form("rdk,da->rka", grid_im, sin_a)
    back_im = mix_form("rdk,da->rka", grid_im, cos_a) + mix_form("rdk,da->rka", grid_re, sin_a)
    twid_cos, twid_sin = twiddle_tables(wide, narrow)
    outer_re = (back_re * twid_cos - back_im * twid_sin).astype(jnp.bfloat16)
    outer_im = (back_im * twid_cos + back_re * twid_sin).astype(jnp.bfloat16)
    real_part = mix_form("rka,kb->rba", outer_re, cos_w) - mix_form("rka,kb->rba", outer_im, sin_w)
    return real_part.reshape(rows_all, length_dft)


def small_mix(table, values):
    return jnp.einsum("gp,cpr->cgr", table.astype(jnp.float32), values.astype(jnp.float32))


def spectral(normed, spectrum, tables, cos_p, sin_p, send_out, send_back):
    col_width, tok_rows = normed.shape
    groups = cos_p.shape[0]
    share = tok_rows // groups
    length_all = tok_rows * groups
    device_pos = lax.axis_index("seq")
    frequency = jnp.arange(tok_rows, dtype=jnp.int32)
    radians = (frequency * device_pos).astype(jnp.float32) * (2.0 * math.pi / length_all)
    twist_cos = jnp.cos(radians)[None, :]
    twist_sin = jnp.sin(radians)[None, :]
    first_re, first_im = forward_local(normed, tables)
    twisted_re = (first_re * twist_cos + first_im * twist_sin).astype(jnp.bfloat16)
    twisted_im = (first_im * twist_cos - first_re * twist_sin).astype(jnp.bfloat16)
    moved_re, moved_im = send_out((twisted_re, twisted_im))
    moved_re = moved_re.reshape(col_width, groups, share)
    moved_im = moved_im.reshape(col_width, groups, share)
    spec_re = small_mix(cos_p, moved_re) + small_mix(sin_p, moved_im)
    spec_im = small_mix(cos_p, moved_im) - small_mix(sin_p, moved_re)
    filter_re = spectrum[0].reshape(col_width, groups, share)
    filter_im = spectrum[1].reshape(col_width, groups, share)
    filtered_re = (filter_re * spec_re - filter_im * spec_im).astype(jnp.bfloat16)
    filtered_im = (filter_re * spec_im + filter_im * spec_re).astype(jnp.bfloat16)
    back_re = small_mix(cos_p, filtered_re) - small_mix(sin_p, filtered_im)
    back_im = small_mix(cos_p, filtered_im) + small_mix(sin_p, filtered_re)
    owned_freq = device_pos * share + jnp.arange(share, dtype=jnp.int32)
    devices = jnp.arange(groups, dtype=jnp.int32)
    undo_radians = (devices[:, None] * owned_freq[None, :]).astype(jnp.float32) * (
        2.0 * math.pi / length_all
    )
    undo_cos = jnp.cos(undo_radians)[None]
    undo_sin = jnp.sin(undo_radians)[None]
    turned_re = (
        (back_re * undo_cos - back_im * undo_sin).astype(jnp.bfloat16).reshape(col_width, tok_rows)
    )
    turned_im = (
        (back_im * undo_cos + back_re * undo_sin).astype(jnp.bfloat16).reshape(col_width, tok_rows)
    )
    home_re, home_im = send_back((turned_re, turned_im))
    return inverse_local(home_re, home_im, tables) * (1.0 / length_all)


MESH = pl.DeviceIdType.MESH
VMEM_BYTES = 56 * 1024 * 1024


def vmem_spec():
    return pl.BlockSpec(memory_space=pltpu.VMEM)


def column_of(row_ref):
    size = row_ref.shape[1]
    shape = (size, size)
    on = lax.broadcasted_iota(jnp.int32, shape, 0) == lax.broadcasted_iota(jnp.int32, shape, 1)
    return jnp.sum(jnp.where(on, row_ref[...], 0.0), axis=1, keepdims=True)


def unfold(flat_ref, wide, out_ref):
    rows, cols = out_ref.shape
    pack = 1 if cols % 128 == 0 else 2
    batch = 8 // pack

    def step(i, carry):
        low = pl.multiple_of(i * (8 * cols), 128)
        for j in range(batch):
            run = flat_ref[0:1, pl.ds(low + j * pack * cols, pack * cols)].astype(jnp.float32)
            for m in range(pack):
                wide[pl.ds(i * 8 + j * pack + m, 1), 0:cols] = run[:, m * cols : (m + 1) * cols]
        return carry

    lax.fori_loop(0, rows // 8, step, 0)
    out_ref[...] = wide[0:rows, 0:cols].astype(jnp.bfloat16)


def greet(axis, n):
    me = lax.axis_index(axis)
    barrier = pltpu.get_barrier_semaphore()
    for k in range(1, n):
        pl.semaphore_signal(
            barrier, inc=1, device_id={axis: lax.rem(me + k, n)}, device_id_type=MESH
        )
    return barrier


def share_stats(n, barrier, stats, send_sem, recv_sem):
    me = lax.axis_index("chan")
    pl.semaphore_wait(barrier, n - 1)
    copies = []
    for k in range(1, n):
        copy = pltpu.make_async_remote_copy(
            src_ref=stats.at[0],
            dst_ref=stats.at[k],
            send_sem=send_sem.at[k],
            recv_sem=recv_sem.at[k],
            device_id={"chan": lax.rem(me + k, n)},
            device_id_type=MESH,
        )
        copy.start()
        copies.append(copy)
    for copy in copies:
        copy.wait()
    total = stats[0]
    for k in range(1, n):
        total = total + stats[k]
    return total


def norm_kernel(n, width, x_ref, gain_ref, out_ref, stats, send_sem, recv_sem):
    barrier = greet("chan", n)
    cols = x_ref.shape[1]
    step = min(cols, 512)
    for c in range(0, cols, step):
        x = x_ref[:, c : c + step].astype(jnp.float32)
        stats[0, 0:1, c : c + step] = jnp.sum(x, axis=0, keepdims=True)
        stats[0, 1:2, c : c + step] = jnp.sum(x * x, axis=0, keepdims=True)
    total = share_stats(n, barrier, stats, send_sem, recv_sem)
    mean = total[0:1] / width
    scale = lax.rsqrt(total[1:2] / width - mean * mean + 1e-05)
    gain = column_of(gain_ref)
    for c in range(0, cols, step):
        x = x_ref[:, c : c + step].astype(jnp.float32)
        y = (x - mean[:, c : c + step]) * scale[:, c : c + step] * gain
        out_ref[:, c : c + step] = y.astype(jnp.bfloat16)


def first_norm(n, width, tokens, gain):
    return pl.pallas_call(
        functools.partial(norm_kernel, n, width),
        out_shape=jax.ShapeDtypeStruct(tokens.shape, jnp.bfloat16),
        in_specs=[vmem_spec()] * 2,
        out_specs=vmem_spec(),
        scratch_shapes=[
            pltpu.VMEM((n, 2, tokens.shape[1]), jnp.float32),
            pltpu.SemaphoreType.DMA((n,)),
            pltpu.SemaphoreType.DMA((n,)),
        ],
        compiler_params=pltpu.CompilerParams(
            collective_id=0, has_side_effects=True, vmem_limit_bytes=VMEM_BYTES
        ),
    )(tokens, gain[None])


def small_dft(values, sign):
    n = len(values)
    if n == 1:
        return values
    even = small_dft(values[0::2], sign)
    odd = small_dft(values[1::2], sign)
    out = [None] * n
    for k in range(n // 2):
        re, im = odd[k]
        if k == 0:
            tr, ti = re, im
        elif 4 * k == n:
            tr, ti = (-im, re) if sign > 0 else (im, -re)
        else:
            c = float(np.float64(math.cos(2 * math.pi * k / n)).astype(jnp.bfloat16))
            s = sign * float(np.float64(math.sin(2 * math.pi * k / n)).astype(jnp.bfloat16))
            tr, ti = re * c - im * s, re * s + im * c
        er, ei = even[k]
        out[k] = (er + tr, ei + ti)
        out[k + n // 2] = (er - tr, ei - ti)
    return out


def conv_kernel(
    n, x_ref, filt_hbm, cos_hbm, sin_hbm, twc_ref, tws_ref, undo_c, undo_s,
    mi_flat, up_flat, down_flat, mo_flat, out_ref, mi_ref, up_ref, down_ref, mo_ref, wide,
    cos_v, sin_v, filt_v, send_f, recv_f, send_b, recv_b,
    load_sem, filt_sem, sf_sem, rf_sem, sb_sem, rb_sem,
):
    me = lax.axis_index("seq")
    barrier = greet("seq", n)
    rows, cols = x_ref.shape
    share = cols // n
    parts = sb_sem.shape[1]
    group = rows // parts

    def block_of(k):
        return pl.ds(pl.multiple_of(lax.rem(me + k, n) * share, share), share)

    def load(k, which):
        hbm, vmem = ((cos_hbm, cos_v), (sin_hbm, sin_v))[which]
        view = block_of(k)
        return pltpu.make_async_copy(hbm.at[:, view], vmem.at[:, view], load_sem.at[k, which])

    filt_copy = pltpu.make_async_copy(filt_hbm, filt_v, filt_sem.at[0])
    for k in list(range(1, n)) + [0]:
        load(k, 0).start()
        load(k, 1).start()
    filt_copy.start()
    pl.semaphore_wait(barrier, n - 1)

    def transform(k):
        load(k, 0).wait()
        load(k, 1).wait()
        view = block_of(k)
        x = x_ref[...]
        re = jnp.dot(x, cos_v[:, view], preferred_element_type=jnp.float32)
        im = -jnp.dot(x, sin_v[:, view], preferred_element_type=jnp.float32)
        tc, ts = twc_ref[:, view], tws_ref[:, view]
        return (
            (re * tc + im * ts).astype(jnp.bfloat16),
            (im * tc - re * ts).astype(jnp.bfloat16),
        )

    def outward(k):
        peer = lax.rem(me + k, n)
        return pltpu.make_async_remote_copy(
            src_ref=send_f.at[k],
            dst_ref=recv_f.at[me],
            send_sem=sf_sem.at[k],
            recv_sem=rf_sem.at[k],
            device_id={"seq": peer},
            device_id_type=MESH,
        )

    def forward(k, carry):
        re, im = transform(k)
        send_f[k, 0] = re
        send_f[k, 1] = im
        outward(k).start()
        return carry

    lax.fori_loop(1, n, forward, 0)
    re, im = transform(0)
    recv_f[me, 0] = re
    recv_f[me, 1] = im
    for flat, square in (
        (mi_flat, mi_ref), (up_flat, up_ref), (down_flat, down_ref), (mo_flat, mo_ref)
    ):
        unfold(flat, wide, square)
    filt_copy.wait()

    def arrive(k, carry):
        outward(k).wait()
        return carry

    lax.fori_loop(1, n, arrive, 0)

    def inward(k, part):
        peer = lax.rem(me + k, n)
        view = pl.ds(part * group, group)
        return pltpu.make_async_remote_copy(
            src_ref=send_b.at[peer, :, view],
            dst_ref=recv_b.at[k, :, view],
            send_sem=sb_sem.at[k, part],
            recv_sem=rb_sem.at[k, part],
            device_id={"seq": peer},
            device_id_type=MESH,
        )

    lanes = 128
    for part in range(parts):

        def middle(i, carry, part=part):
            view = pl.ds(pl.multiple_of(part * group + i * 16, 16), 16)
            for c in range(0, share, lanes):
                values = [
                    (
                        recv_f[p, 0, view, c : c + lanes].astype(jnp.float32),
                        recv_f[p, 1, view, c : c + lanes].astype(jnp.float32),
                    )
                    for p in range(n)
                ]
                spec = small_dft(values, -1)
                filtered = []
                for g in range(n):
                    sr, si = spec[g]
                    low = g * share + c
                    fr = filt_v[0, view, low : low + lanes]
                    fi = filt_v[1, view, low : low + lanes]
                    filtered.append((fr * sr - fi * si, fr * si + fi * sr))
                back = small_dft(filtered, 1)
                for p in range(n):
                    br, bi = back[p]
                    uc = undo_c[p : p + 1, c : c + lanes]
                    us = undo_s[p : p + 1, c : c + lanes]
                    send_b[p, 0, view, c : c + lanes] = (br * uc - bi * us).astype(jnp.bfloat16)
                    send_b[p, 1, view, c : c + lanes] = (bi * uc + br * us).astype(jnp.bfloat16)
            return carry

        lax.fori_loop(0, group // 16, middle, 0)

        def push(k, carry, part=part):
            inward(k, part).start()
            return carry

        lax.fori_loop(1, n, push, 0)

    tile = min(cols, 512)
    scale = 1.0 / (n * cols)

    def accumulate(re, im, source, first):
        view = pl.ds(pl.multiple_of(source * share, share), share)

        def column(t, carry):
            low = pl.ds(pl.multiple_of(t * tile, tile), tile)
            term = jnp.dot(re, cos_v[view, low], preferred_element_type=jnp.float32) - jnp.dot(
                im, sin_v[view, low], preferred_element_type=jnp.float32
            )
            if first:
                out_ref[:, low] = term * scale
            else:
                out_ref[:, low] += term * scale
            return carry

        lax.fori_loop(0, cols // tile, column, 0)

    accumulate(send_b[me, 0], send_b[me, 1], me, True)

    def back_step(k, carry):
        for part in range(parts):
            inward(k, part).wait()
        accumulate(recv_b[k, 0], recv_b[k, 1], lax.rem(me + n - k, n), False)
        return carry

    lax.fori_loop(1, n, back_step, 0)


def convolve_kernel(n, normed, spectrum, flats):
    rows, cols = normed.shape
    hidden = flats[1].shape[1] // rows
    shapes = [(rows, rows), (rows, hidden), (hidden, rows), (rows, rows)]
    share = cols // n
    index = np.arange(cols)
    angle = (index[:, None] * index[None, :] % cols) * (2.0 * math.pi / cols)
    cos_m = jnp.asarray(np.cos(angle).astype(jnp.bfloat16))
    sin_m = jnp.asarray(np.sin(angle).astype(jnp.bfloat16))
    pos = lax.axis_index("seq")
    turn = 2.0 * math.pi / (n * cols)
    twist = (jnp.arange(cols, dtype=jnp.int32) * pos).astype(jnp.float32)[None] * turn
    owned = pos * share + jnp.arange(share, dtype=jnp.int32)
    undo = (jnp.arange(n, dtype=jnp.int32)[:, None] * owned[None]).astype(jnp.float32) * turn
    parts = 4 if rows % 64 == 0 else 1
    block = pltpu.VMEM((n, 2, rows, share), jnp.bfloat16)
    dma = pltpu.SemaphoreType.DMA
    return pl.pallas_call(
        functools.partial(conv_kernel, n),
        out_shape=[jax.ShapeDtypeStruct((rows, cols), jnp.float32)]
        + [jax.ShapeDtypeStruct(shape, jnp.bfloat16) for shape in shapes],
        in_specs=[vmem_spec()] + [pl.BlockSpec(memory_space=pl.ANY)] * 3 + [vmem_spec()] * 8,
        out_specs=[vmem_spec()] * 5,
        scratch_shapes=[
            pltpu.VMEM((max(rows, hidden),) * 2, jnp.float32),
            pltpu.VMEM((cols, cols), jnp.bfloat16),
            pltpu.VMEM((cols, cols), jnp.bfloat16),
            pltpu.VMEM(spectrum.shape, jnp.float32),
            block, block, block, block,
            dma((n, 2)), dma((1,)), dma((n,)), dma((n,)), dma((n, parts)), dma((n, parts)),
        ],
        compiler_params=pltpu.CompilerParams(
            collective_id=1, has_side_effects=True, vmem_limit_bytes=VMEM_BYTES
        ),
    )(normed, spectrum, cos_m, sin_m, jnp.cos(twist), jnp.sin(twist), jnp.cos(undo), jnp.sin(undo), *flats)


def across(left, right):
    return lax.dot_general(
        left, right, (((0,), (0,)), ((), ())), preferred_element_type=jnp.float32
    )


def mlp_kernel(
    n, width, tok_ref, conv_ref, norm_ref, skip_ref, gain_ref, mi_ref, up_ref, down_ref, mo_ref,
    out_ref, resid, stats, first, regrouped, lowered, returned,
    st_send, st_recv, send_sem, recv_sem,
):
    me = lax.axis_index("chan")
    barrier = greet("chan", n)
    rows, cols = tok_ref.shape
    chunks, _, step = first.shape
    piece = rows // n
    skip, gain = column_of(skip_ref), column_of(gain_ref)

    def residual_of(c, carry):
        view = pl.ds(pl.multiple_of(c * step, step), step)
        value = (
            tok_ref[:, view].astype(jnp.float32)
            + conv_ref[:, view]
            + skip * norm_ref[:, view].astype(jnp.float32)
        ).astype(jnp.bfloat16)
        resid[:, view] = value
        value = value.astype(jnp.float32)
        stats[0, 0:1, view] = jnp.sum(value, axis=0, keepdims=True)
        stats[0, 1:2, view] = jnp.sum(value * value, axis=0, keepdims=True)
        return carry

    lax.fori_loop(0, chunks, residual_of, 0)
    total = share_stats(n, barrier, stats, st_send, st_recv)
    mean = total[0:1] / width
    stats[0, 0:1, :] = mean
    stats[0, 1:2, :] = lax.rsqrt(total[1:2] / width - mean * mean + 1e-05)

    def exchange(phase, c, k):
        peer = lax.rem(me + k, n)
        source, target = ((first, regrouped), (lowered, returned))[phase]
        return pltpu.make_async_remote_copy(
            src_ref=source.at[c, pl.ds(pl.multiple_of(peer * piece, 16), piece)],
            dst_ref=target.at[c, pl.ds(pl.multiple_of(me * piece, 16), piece)],
            send_sem=send_sem.at[phase, c, k],
            recv_sem=recv_sem.at[phase, c, k],
            device_id={"chan": peer},
            device_id_type=MESH,
        )

    own = pl.ds(pl.multiple_of(me * piece, 16), piece)

    def first_step(c, carry):
        view = pl.ds(pl.multiple_of(c * step, step), step)
        value = resid[:, view].astype(jnp.float32)
        value = (value - stats[0, 0:1, view]) * stats[0, 1:2, view] * gain
        first[c] = across(mi_ref[...], value.astype(jnp.bfloat16)).astype(jnp.bfloat16)
        for k in range(1, n):
            exchange(0, c, k).start()
        regrouped[c, own] = first[c, own]
        return carry

    lax.fori_loop(0, chunks, first_step, 0)

    def second_step(c, carry):
        for k in range(1, n):
            exchange(0, c, k).wait()
        pre = across(up_ref[...], regrouped[c])
        hidden = 0.5 * pre * (1.0 + lax.erf(pre * math.sqrt(0.5)))
        lowered[c] = across(down_ref[...], hidden.astype(jnp.bfloat16)).astype(jnp.bfloat16)
        for k in range(1, n):
            exchange(1, c, k).start()
        returned[c, own] = lowered[c, own]
        return carry

    lax.fori_loop(0, chunks, second_step, 0)

    def third_step(c, carry):
        view = pl.ds(pl.multiple_of(c * step, step), step)
        for k in range(1, n):
            exchange(1, c, k).wait()
        term = across(mo_ref[...], returned[c])
        out_ref[:, view] = (resid[:, view].astype(jnp.float32) + term).astype(jnp.bfloat16)
        return carry

    lax.fori_loop(0, chunks, third_step, 0)


def mlp(n, width, *operands):
    rows, cols = operands[0].shape
    step = 256 if cols % 256 == 0 else cols
    chunks = cols // step
    block = pltpu.VMEM((chunks, rows, step), jnp.bfloat16)
    dma = pltpu.SemaphoreType.DMA
    return pl.pallas_call(
        functools.partial(mlp_kernel, n, width),
        out_shape=jax.ShapeDtypeStruct((rows, cols), jnp.bfloat16),
        in_specs=[vmem_spec()] * len(operands),
        out_specs=vmem_spec(),
        scratch_shapes=[
            pltpu.VMEM((rows, cols), jnp.bfloat16),
            pltpu.VMEM((n, 2, cols), jnp.float32),
            block, block, block, block,
            dma((n,)), dma((n,)), dma((2, chunks, n)), dma((2, chunks, n)),
        ],
        compiler_params=pltpu.CompilerParams(
            collective_id=2, has_side_effects=True, vmem_limit_bytes=VMEM_BYTES
        ),
    )(*operands)


def shards(
    tokens,
    filter_spectrum,
    skip_weight,
    norm_gain,
    mlp_gain,
    mix_in,
    up_weight,
    down_weight,
    mix_out,
):
    columns, tok_rows = tokens.shape
    groups = lax.axis_size("seq")
    blocks = lax.axis_size("chan")
    width = columns * blocks
    normed = first_norm(blocks, width, tokens, norm_gain)
    hidden_width = up_weight.shape[1] // columns
    flats = (mix_in, up_weight, down_weight, mix_out)
    if groups == 8 and (tok_rows // groups) % 128 == 0:
        convolved, *factors = convolve_kernel(groups, normed, filter_spectrum, flats)
    else:
        cos_w, sin_w = dft_tables(RADIX)
        cos_a, sin_a = dft_tables(tok_rows // RADIX)
        cos_p, sin_p = dft_tables(groups)

        def swap(pair_in):
            return tuple(
                lax.all_to_all(half, "seq", split_axis=1, concat_axis=1, tiled=True)
                for half in pair_in
            )

        convolved = spectral(
            normed, filter_spectrum, (cos_w, sin_w, cos_a, sin_a), cos_p, sin_p, swap, swap
        )
        shapes = ((columns, columns), (columns, hidden_width), (hidden_width, columns))
        factors = [flat.reshape(shape) for flat, shape in zip(flats, shapes + shapes[:1])]
    return mlp(
        blocks,
        width,
        tokens,
        convolved,
        normed,
        skip_weight[None],
        mlp_gain[None],
        *factors,
    )


def solution(mesh):
    in_specs = (
        P("chan", "seq"),
        P(None, "chan", "seq"),
        P("chan"),
        P("chan"),
        P("chan"),
        P("chan", None),
        P("chan", None),
        P("chan", None),
        P("chan", None),
    )
    out_specs = P("chan", "seq")
    return jax.shard_map(shards, mesh=mesh, in_specs=in_specs, out_specs=out_specs, check_vma=False)
```

```python
import functools
import math

import jax
import jax.numpy as jnp
import numpy as np
from jax import lax
from jax.experimental import pallas as pl
from jax.experimental.pallas import tpu as pltpu
from jax.sharding import PartitionSpec as P

RADIX = 64


def dft_tables(length_dft):
    position = jnp.arange(length_dft, dtype=jnp.int32)
    phase_int = position[:, None] * position[None, :] % length_dft
    radians = phase_int.astype(jnp.float32) * (2.0 * math.pi / length_dft)
    return (jnp.cos(radians).astype(jnp.bfloat16), jnp.sin(radians).astype(jnp.bfloat16))


def twiddle_tables(wide, narrow):
    outer_idx = jnp.arange(wide, dtype=jnp.int32)
    inner_idx = jnp.arange(narrow, dtype=jnp.int32)
    phase_int = outer_idx[:, None] * inner_idx[None, :] % (wide * narrow)
    radians = phase_int.astype(jnp.float32) * (2.0 * math.pi / (wide * narrow))
    return (jnp.cos(radians)[None], jnp.sin(radians)[None])


def mix_form(form, left_op, right_op):
    return jnp.einsum(form, left_op.astype(jnp.float32), right_op.astype(jnp.float32))


def forward_local(values, tables):
    cos_w, sin_w, cos_a, sin_a = tables
    rows_all, length_dft = values.shape
    wide = cos_w.shape[0]
    narrow = length_dft // wide
    grid = values.reshape(rows_all, wide, narrow)
    section_re = mix_form("rba,bk->rka", grid, cos_w)
    section_im = -mix_form("rba,bk->rka", grid, sin_w)
    twid_cos, twid_sin = twiddle_tables(wide, narrow)
    inner_re = (section_re * twid_cos + section_im * twid_sin).astype(jnp.bfloat16)
    inner_im = (section_im * twid_cos - section_re * twid_sin).astype(jnp.bfloat16)
    out_re = mix_form("rka,ad->rdk", inner_re, cos_a) + mix_form("rka,ad->rdk", inner_im, sin_a)
    out_im = mix_form("rka,ad->rdk", inner_im, cos_a) - mix_form("rka,ad->rdk", inner_re, sin_a)
    return (out_re.reshape(rows_all, length_dft), out_im.reshape(rows_all, length_dft))


def inverse_local(values_re, values_im, tables):
    cos_w, sin_w, cos_a, sin_a = tables
    rows_all, length_dft = values_re.shape
    wide = cos_w.shape[0]
    narrow = length_dft // wide
    grid_re = values_re.reshape(rows_all, narrow, wide)
    grid_im = values_im.reshape(rows_all, narrow, wide)
    back_re = mix_form("rdk,da->rka", grid_re, cos_a) - mix_form("rdk,da->rka", grid_im, sin_a)
    back_im = mix_form("rdk,da->rka", grid_im, cos_a) + mix_form("rdk,da->rka", grid_re, sin_a)
    twid_cos, twid_sin = twiddle_tables(wide, narrow)
    outer_re = (back_re * twid_cos - back_im * twid_sin).astype(jnp.bfloat16)
    outer_im = (back_im * twid_cos + back_re * twid_sin).astype(jnp.bfloat16)
    real_part = mix_form("rka,kb->rba", outer_re, cos_w) - mix_form("rka,kb->rba", outer_im, sin_w)
    return real_part.reshape(rows_all, length_dft)


def small_mix(table, values):
    return jnp.einsum("gp,cpr->cgr", table.astype(jnp.float32), values.astype(jnp.float32))


def spectral(normed, spectrum, tables, cos_p, sin_p, send_out, send_back):
    col_width, tok_rows = normed.shape
    groups = cos_p.shape[0]
    share = tok_rows // groups
    length_all = tok_rows * groups
    device_pos = lax.axis_index("seq")
    frequency = jnp.arange(tok_rows, dtype=jnp.int32)
    radians = (frequency * device_pos).astype(jnp.float32) * (2.0 * math.pi / length_all)
    twist_cos = jnp.cos(radians)[None, :]
    twist_sin = jnp.sin(radians)[None, :]
    first_re, first_im = forward_local(normed, tables)
    twisted_re = (first_re * twist_cos + first_im * twist_sin).astype(jnp.bfloat16)
    twisted_im = (first_im * twist_cos - first_re * twist_sin).astype(jnp.bfloat16)
    moved_re, moved_im = send_out((twisted_re, twisted_im))
    moved_re = moved_re.reshape(col_width, groups, share)
    moved_im = moved_im.reshape(col_width, groups, share)
    spec_re = small_mix(cos_p, moved_re) + small_mix(sin_p, moved_im)
    spec_im = small_mix(cos_p, moved_im) - small_mix(sin_p, moved_re)
    filter_re = spectrum[0].reshape(col_width, groups, share)
    filter_im = spectrum[1].reshape(col_width, groups, share)
    filtered_re = (filter_re * spec_re - filter_im * spec_im).astype(jnp.bfloat16)
    filtered_im = (filter_re * spec_im + filter_im * spec_re).astype(jnp.bfloat16)
    back_re = small_mix(cos_p, filtered_re) - small_mix(sin_p, filtered_im)
    back_im = small_mix(cos_p, filtered_im) + small_mix(sin_p, filtered_re)
    owned_freq = device_pos * share + jnp.arange(share, dtype=jnp.int32)
    devices = jnp.arange(groups, dtype=jnp.int32)
    undo_radians = (devices[:, None] * owned_freq[None, :]).astype(jnp.float32) * (
        2.0 * math.pi / length_all
    )
    undo_cos = jnp.cos(undo_radians)[None]
    undo_sin = jnp.sin(undo_radians)[None]
    turned_re = (
        (back_re * undo_cos - back_im * undo_sin).astype(jnp.bfloat16).reshape(col_width, tok_rows)
    )
    turned_im = (
        (back_im * undo_cos + back_re * undo_sin).astype(jnp.bfloat16).reshape(col_width, tok_rows)
    )
    home_re, home_im = send_back((turned_re, turned_im))
    return inverse_local(home_re, home_im, tables) * (1.0 / length_all)


MESH = pl.DeviceIdType.MESH
VMEM_BYTES = 56 * 1024 * 1024


def vmem_spec():
    return pl.BlockSpec(memory_space=pltpu.VMEM)


def column_of(row_ref):
    size = row_ref.shape[1]
    shape = (size, size)
    on = lax.broadcasted_iota(jnp.int32, shape, 0) == lax.broadcasted_iota(jnp.int32, shape, 1)
    return jnp.sum(jnp.where(on, row_ref[...], 0.0), axis=1, keepdims=True)


def unfold(flat_ref, wide, out_ref):
    rows, cols = out_ref.shape
    pack = 1 if cols % 128 == 0 else 2
    batch = 8 // pack

    def step(i, carry):
        low = pl.multiple_of(i * (8 * cols), 128)
        for j in range(batch):
            run = flat_ref[0:1, pl.ds(low + j * pack * cols, pack * cols)].astype(jnp.float32)
            for m in range(pack):
                wide[pl.ds(i * 8 + j * pack + m, 1), 0:cols] = run[:, m * cols : (m + 1) * cols]
        return carry

    lax.fori_loop(0, rows // 8, step, 0)
    out_ref[...] = wide[0:rows, 0:cols].astype(jnp.bfloat16)


def greet(axis, n):
    me = lax.axis_index(axis)
    barrier = pltpu.get_barrier_semaphore()
    for k in range(1, n):
        pl.semaphore_signal(
            barrier, inc=1, device_id={axis: lax.rem(me + k, n)}, device_id_type=MESH
        )
    return barrier


def share_stats(n, stats, send_sem, recv_sem):
    me = lax.axis_index("chan")
    copies = []
    for k in range(1, n):
        copy = pltpu.make_async_remote_copy(
            src_ref=stats.at[0],
            dst_ref=stats.at[k],
            send_sem=send_sem.at[k],
            recv_sem=recv_sem.at[k],
            device_id={"chan": lax.rem(me + k, n)},
            device_id_type=MESH,
        )
        copy.start()
        copies.append(copy)
    for copy in copies:
        copy.wait()
    total = stats[0]
    for k in range(1, n):
        total = total + stats[k]
    return total


def norm_kernel(n, width, x_ref, gain_ref, out_ref, stats, send_sem, recv_sem):
    barrier = greet("chan", n)
    norm_body(n, width, barrier, n - 1, x_ref, gain_ref, out_ref, stats, send_sem, recv_sem)


def norm_body(n, width, barrier, signals, x_ref, gain_ref, out_ref, stats, send_sem, recv_sem):
    cols = x_ref.shape[1]
    step = min(cols, 512)
    for c in range(0, cols, step):
        x = x_ref[:, c : c + step].astype(jnp.float32)
        stats[0, 0:1, c : c + step] = jnp.sum(x, axis=0, keepdims=True)
        stats[0, 1:2, c : c + step] = jnp.sum(x * x, axis=0, keepdims=True)
    pl.semaphore_wait(barrier, signals)
    total = share_stats(n, stats, send_sem, recv_sem)
    mean = total[0:1] / width
    scale = lax.rsqrt(total[1:2] / width - mean * mean + 1e-05)
    gain = column_of(gain_ref)
    for c in range(0, cols, step):
        x = x_ref[:, c : c + step].astype(jnp.float32)
        y = (x - mean[:, c : c + step]) * scale[:, c : c + step] * gain
        out_ref[:, c : c + step] = y.astype(jnp.bfloat16)


def first_norm(n, width, tokens, gain):
    return pl.pallas_call(
        functools.partial(norm_kernel, n, width),
        out_shape=jax.ShapeDtypeStruct(tokens.shape, jnp.bfloat16),
        in_specs=[vmem_spec()] * 2,
        out_specs=vmem_spec(),
        scratch_shapes=[
            pltpu.VMEM((n, 2, tokens.shape[1]), jnp.float32),
            pltpu.SemaphoreType.DMA((n,)),
            pltpu.SemaphoreType.DMA((n,)),
        ],
        compiler_params=pltpu.CompilerParams(
            collective_id=0, has_side_effects=True, vmem_limit_bytes=VMEM_BYTES
        ),
    )(tokens, gain[None])


def small_dft(values, sign):
    n = len(values)
    if n == 1:
        return values
    even = small_dft(values[0::2], sign)
    odd = small_dft(values[1::2], sign)
    out = [None] * n
    for k in range(n // 2):
        re, im = odd[k]
        if k == 0:
            tr, ti = re, im
        elif 4 * k == n:
            tr, ti = (-im, re) if sign > 0 else (im, -re)
        else:
            c = float(np.float64(math.cos(2 * math.pi * k / n)).astype(jnp.bfloat16))
            s = sign * float(np.float64(math.sin(2 * math.pi * k / n)).astype(jnp.bfloat16))
            tr, ti = re * c - im * s, re * s + im * c
        er, ei = even[k]
        out[k] = (er + tr, ei + ti)
        out[k + n // 2] = (er - tr, ei - ti)
    return out


def conv_kernel(
    n, n_chan, width, tok_ref, gain_ref, filt_hbm, cos_hbm, sin_hbm,
    twc_ref, tws_ref, undo_c, undo_s,
    mi_flat, up_flat, down_flat, mo_flat,
    out_ref, x_ref, mi_ref, up_ref, down_ref, mo_ref, wide,
    cos_v, sin_v, filt_v, send_f, recv_f, send_b, recv_b, stats,
    st_send, st_recv, load_sem, filt_sem, sf_sem, rf_sem, sb_sem, rb_sem,
):
    me = lax.axis_index("seq")
    barrier = greet("seq", n)
    greet("chan", n_chan)
    rows, cols = x_ref.shape
    share = cols // n
    parts = sb_sem.shape[1]
    group = rows // parts

    def block_of(k):
        return pl.ds(pl.multiple_of(lax.rem(me + k, n) * share, share), share)

    def load(k, which):
        hbm, vmem = ((cos_hbm, cos_v), (sin_hbm, sin_v))[which]
        view = block_of(k)
        return pltpu.make_async_copy(hbm.at[:, view], vmem.at[:, view], load_sem.at[k, which])

    filt_copy = pltpu.make_async_copy(filt_hbm, filt_v, filt_sem.at[0])
    for k in list(range(1, n)) + [0]:
        load(k, 0).start()
        load(k, 1).start()
    filt_copy.start()
    norm_body(
        n_chan, width, barrier, n + n_chan - 2, tok_ref, gain_ref, x_ref, stats, st_send, st_recv
    )

    def transform(k, part):
        if part == 0:
            load(k, 0).wait()
            load(k, 1).wait()
        view = block_of(k)
        x = x_ref[part * group : (part + 1) * group, :]
        re = jnp.dot(x, cos_v[:, view], preferred_element_type=jnp.float32)
        im = -jnp.dot(x, sin_v[:, view], preferred_element_type=jnp.float32)
        tc, ts = twc_ref[me, :, view], tws_ref[me, :, view]
        return (
            (re * tc + im * ts).astype(jnp.bfloat16),
            (im * tc - re * ts).astype(jnp.bfloat16),
        )

    def rows_of(part):
        return pl.ds(part * group, group)

    def outward(k, part):
        return pltpu.make_async_remote_copy(
            src_ref=send_f.at[k, :, rows_of(part)],
            dst_ref=recv_f.at[me, :, rows_of(part)],
            send_sem=sf_sem.at[k, part],
            recv_sem=rf_sem.at[k, part],
            device_id={"seq": lax.rem(me + k, n)},
            device_id_type=MESH,
        )

    for part in range(parts):

        def forward(k, carry, part=part):
            re, im = transform(k, part)
            send_f[k, 0, rows_of(part)] = re
            send_f[k, 1, rows_of(part)] = im
            outward(k, part).start()
            return carry

        lax.fori_loop(1, n, forward, 0)
        re, im = transform(0, part)
        recv_f[me, 0, rows_of(part)] = re
        recv_f[me, 1, rows_of(part)] = im
    filt_copy.wait()

    def inward(k, part):
        peer = lax.rem(me + k, n)
        return pltpu.make_async_remote_copy(
            src_ref=send_b.at[peer, :, rows_of(part)],
            dst_ref=recv_b.at[k, :, rows_of(part)],
            send_sem=sb_sem.at[k, part],
            recv_sem=rb_sem.at[k, part],
            device_id={"seq": peer},
            device_id_type=MESH,
        )

    lanes = 128
    for part in range(parts):

        def arrive(k, carry, part=part):
            outward(k, part).wait()
            return carry

        lax.fori_loop(1, n, arrive, 0)

        def middle(i, carry, part=part):
            view = pl.ds(pl.multiple_of(part * group + i * 16, 16), 16)
            for c in range(0, share, lanes):
                values = [
                    (
                        recv_f[p, 0, view, c : c + lanes].astype(jnp.float32),
                        recv_f[p, 1, view, c : c + lanes].astype(jnp.float32),
                    )
                    for p in range(n)
                ]
                spec = small_dft(values, -1)
                filtered = []
                for g in range(n):
                    sr, si = spec[g]
                    low = g * share + c
                    fr = filt_v[0, view, low : low + lanes]
                    fi = filt_v[1, view, low : low + lanes]
                    filtered.append((fr * sr - fi * si, fr * si + fi * sr))
                back = small_dft(filtered, 1)
                for p in range(n):
                    br, bi = back[p]
                    uc = undo_c[me, p : p + 1, c : c + lanes]
                    us = undo_s[me, p : p + 1, c : c + lanes]
                    send_b[p, 0, view, c : c + lanes] = (br * uc - bi * us).astype(jnp.bfloat16)
                    send_b[p, 1, view, c : c + lanes] = (bi * uc + br * us).astype(jnp.bfloat16)
            return carry

        lax.fori_loop(0, group // 16, middle, 0)

        def push(k, carry, part=part):
            inward(k, part).start()
            return carry

        lax.fori_loop(1, n, push, 0)

    for flat, square in (
        (mi_flat, mi_ref), (up_flat, up_ref), (down_flat, down_ref), (mo_flat, mo_ref)
    ):
        unfold(flat, wide, square)

    tile = min(cols, 512)
    scale = 1.0 / (n * cols)

    def accumulate(re, im, source, part, first):
        view = pl.ds(pl.multiple_of(source * share, share), share)

        def column(t, carry):
            low = pl.ds(pl.multiple_of(t * tile, tile), tile)
            term = jnp.dot(re, cos_v[view, low], preferred_element_type=jnp.float32) - jnp.dot(
                im, sin_v[view, low], preferred_element_type=jnp.float32
            )
            if first:
                out_ref[rows_of(part), low] = term * scale
            else:
                out_ref[rows_of(part), low] += term * scale
            return carry

        lax.fori_loop(0, cols // tile, column, 0)

    for part in range(parts):
        accumulate(send_b[me, 0, rows_of(part)], send_b[me, 1, rows_of(part)], me, part, True)
    for part in range(parts):

        def back_step(k, carry, part=part):
            inward(k, part).wait()
            source = lax.rem(me + n - k, n)
            accumulate(
                recv_b[k, 0, rows_of(part)], recv_b[k, 1, rows_of(part)], source, part, False
            )
            return carry

        lax.fori_loop(1, n, back_step, 0)


def convolve_kernel(n, n_chan, width, tokens, gain, spectrum, flats):
    rows, cols = tokens.shape
    hidden = flats[1].shape[1] // rows
    shapes = [(rows, cols), (rows, rows), (rows, hidden), (hidden, rows), (rows, rows)]
    share = cols // n
    index = np.arange(cols)
    angle = (index[:, None] * index[None, :] % cols) * (2.0 * math.pi / cols)
    cos_m = jnp.asarray(np.cos(angle).astype(jnp.bfloat16))
    sin_m = jnp.asarray(np.sin(angle).astype(jnp.bfloat16))
    turn = 2.0 * math.pi / (n * cols)
    ranks = np.arange(n)
    twist = ranks[:, None, None] * index[None, None, :] * turn
    owned = ranks[:, None] * share + np.arange(share)[None]
    undo = ranks[None, :, None] * owned[:, None, :] * turn
    small = [
        jnp.asarray(form(angles).astype(np.float32))
        for angles in (twist, undo)
        for form in (np.cos, np.sin)
    ]
    parts = 2 if rows % 32 == 0 else 1
    block = pltpu.VMEM((n, 2, rows, share), jnp.bfloat16)
    dma = pltpu.SemaphoreType.DMA
    pair = dma((n, parts))
    return pl.pallas_call(
        functools.partial(conv_kernel, n, n_chan, width),
        out_shape=[jax.ShapeDtypeStruct((rows, cols), jnp.float32)]
        + [jax.ShapeDtypeStruct(shape, jnp.bfloat16) for shape in shapes],
        in_specs=[vmem_spec()] * 2 + [pl.BlockSpec(memory_space=pl.ANY)] * 3 + [vmem_spec()] * 8,
        out_specs=[vmem_spec()] * 6,
        scratch_shapes=[
            pltpu.VMEM((max(rows, hidden),) * 2, jnp.float32),
            pltpu.VMEM((cols, cols), jnp.bfloat16),
            pltpu.VMEM((cols, cols), jnp.bfloat16),
            pltpu.VMEM(spectrum.shape, jnp.float32),
            block, block, block, block,
            pltpu.VMEM((n_chan, 2, cols), jnp.float32),
            dma((n_chan,)), dma((n_chan,)), dma((n, 2)), dma((1,)), pair, pair, pair, pair,
        ],
        compiler_params=pltpu.CompilerParams(
            collective_id=1, has_side_effects=True, vmem_limit_bytes=VMEM_BYTES
        ),
    )(tokens, gain[None], spectrum, cos_m, sin_m, *small, *flats)


def across(left, right):
    return lax.dot_general(
        left, right, (((0,), (0,)), ((), ())), preferred_element_type=jnp.float32
    )


def mlp_kernel(
    n, width, tok_ref, conv_ref, norm_ref, skip_ref, gain_ref, mi_ref, up_ref, down_ref, mo_ref,
    out_ref, resid, stats, first, regrouped, lowered, returned,
    st_send, st_recv, send_sem, recv_sem,
):
    me = lax.axis_index("chan")
    barrier = greet("chan", n)
    rows, cols = tok_ref.shape
    chunks, _, step = first.shape
    piece = rows // n
    skip, gain = column_of(skip_ref), column_of(gain_ref)

    def residual_of(c, carry):
        view = pl.ds(pl.multiple_of(c * step, step), step)
        value = (
            tok_ref[:, view].astype(jnp.float32)
            + conv_ref[:, view]
            + skip * norm_ref[:, view].astype(jnp.float32)
        ).astype(jnp.bfloat16)
        resid[:, view] = value
        value = value.astype(jnp.float32)
        stats[0, 0:1, view] = jnp.sum(value, axis=0, keepdims=True)
        stats[0, 1:2, view] = jnp.sum(value * value, axis=0, keepdims=True)
        return carry

    lax.fori_loop(0, chunks, residual_of, 0)
    pl.semaphore_wait(barrier, n - 1)
    total = share_stats(n, stats, st_send, st_recv)
    mean = total[0:1] / width
    stats[0, 0:1, :] = mean
    stats[0, 1:2, :] = lax.rsqrt(total[1:2] / width - mean * mean + 1e-05)

    def exchange(phase, c, k):
        peer = lax.rem(me + k, n)
        source, target = ((first, regrouped), (lowered, returned))[phase]
        return pltpu.make_async_remote_copy(
            src_ref=source.at[c, pl.ds(pl.multiple_of(peer * piece, 16), piece)],
            dst_ref=target.at[c, pl.ds(pl.multiple_of(me * piece, 16), piece)],
            send_sem=send_sem.at[phase, c, k],
            recv_sem=recv_sem.at[phase, c, k],
            device_id={"chan": peer},
            device_id_type=MESH,
        )

    own = pl.ds(pl.multiple_of(me * piece, 16), piece)

    def first_step(c, carry):
        view = pl.ds(pl.multiple_of(c * step, step), step)
        value = resid[:, view].astype(jnp.float32)
        value = (value - stats[0, 0:1, view]) * stats[0, 1:2, view] * gain
        first[c] = across(mi_ref[...], value.astype(jnp.bfloat16)).astype(jnp.bfloat16)
        for k in range(1, n):
            exchange(0, c, k).start()
        regrouped[c, own] = first[c, own]
        return carry

    lax.fori_loop(0, chunks, first_step, 0)

    def second_step(c, carry):
        for k in range(1, n):
            exchange(0, c, k).wait()
        pre = across(up_ref[...], regrouped[c])
        hidden = 0.5 * pre * (1.0 + lax.erf(pre * math.sqrt(0.5)))
        lowered[c] = across(down_ref[...], hidden.astype(jnp.bfloat16)).astype(jnp.bfloat16)
        for k in range(1, n):
            exchange(1, c, k).start()
        returned[c, own] = lowered[c, own]
        return carry

    lax.fori_loop(0, chunks, second_step, 0)

    def third_step(c, carry):
        view = pl.ds(pl.multiple_of(c * step, step), step)
        for k in range(1, n):
            exchange(1, c, k).wait()
        term = across(mo_ref[...], returned[c])
        out_ref[:, view] = (resid[:, view].astype(jnp.float32) + term).astype(jnp.bfloat16)
        return carry

    lax.fori_loop(0, chunks, third_step, 0)


def mlp(n, width, *operands):
    rows, cols = operands[0].shape
    step = 256 if cols % 256 == 0 else cols
    chunks = cols // step
    block = pltpu.VMEM((chunks, rows, step), jnp.bfloat16)
    dma = pltpu.SemaphoreType.DMA
    return pl.pallas_call(
        functools.partial(mlp_kernel, n, width),
        out_shape=jax.ShapeDtypeStruct((rows, cols), jnp.bfloat16),
        in_specs=[vmem_spec()] * len(operands),
        out_specs=vmem_spec(),
        scratch_shapes=[
            pltpu.VMEM((rows, cols), jnp.bfloat16),
            pltpu.VMEM((n, 2, cols), jnp.float32),
            block, block, block, block,
            dma((n,)), dma((n,)), dma((2, chunks, n)), dma((2, chunks, n)),
        ],
        compiler_params=pltpu.CompilerParams(
            collective_id=2, has_side_effects=True, vmem_limit_bytes=VMEM_BYTES
        ),
    )(*operands)


def shards(
    tokens,
    filter_spectrum,
    skip_weight,
    norm_gain,
    mlp_gain,
    mix_in,
    up_weight,
    down_weight,
    mix_out,
):
    columns, tok_rows = tokens.shape
    groups = lax.axis_size("seq")
    blocks = lax.axis_size("chan")
    width = columns * blocks
    hidden_width = up_weight.shape[1] // columns
    flats = (mix_in, up_weight, down_weight, mix_out)
    if groups == 8 and (tok_rows // groups) % 128 == 0:
        convolved, normed, *factors = convolve_kernel(
            groups, blocks, width, tokens, norm_gain, filter_spectrum, flats
        )
    else:
        normed = first_norm(blocks, width, tokens, norm_gain)
        cos_w, sin_w = dft_tables(RADIX)
        cos_a, sin_a = dft_tables(tok_rows // RADIX)
        cos_p, sin_p = dft_tables(groups)

        def swap(pair_in):
            return tuple(
                lax.all_to_all(half, "seq", split_axis=1, concat_axis=1, tiled=True)
                for half in pair_in
            )

        convolved = spectral(
            normed, filter_spectrum, (cos_w, sin_w, cos_a, sin_a), cos_p, sin_p, swap, swap
        )
        shapes = ((columns, columns), (columns, hidden_width), (hidden_width, columns))
        factors = [flat.reshape(shape) for flat, shape in zip(flats, shapes + shapes[:1])]
    return mlp(
        blocks,
        width,
        tokens,
        convolved,
        normed,
        skip_weight[None],
        mlp_gain[None],
        *factors,
    )


def solution(mesh):
    in_specs = (
        P("chan", "seq"),
        P(None, "chan", "seq"),
        P("chan"),
        P("chan"),
        P("chan"),
        P("chan", None),
        P("chan", None),
        P("chan", None),
        P("chan", None),
    )
    out_specs = P("chan", "seq")
    return jax.shard_map(shards, mesh=mesh, in_specs=in_specs, out_specs=out_specs, check_vma=False)
```

```python
import functools
import math

import jax
import jax.numpy as jnp
import numpy as np
from jax import lax
from jax.experimental import pallas as pl
from jax.experimental.pallas import tpu as pltpu
from jax.sharding import PartitionSpec as P

RADIX = 64


def dft_tables(length_dft):
    position = jnp.arange(length_dft, dtype=jnp.int32)
    phase_int = position[:, None] * position[None, :] % length_dft
    radians = phase_int.astype(jnp.float32) * (2.0 * math.pi / length_dft)
    return (jnp.cos(radians).astype(jnp.bfloat16), jnp.sin(radians).astype(jnp.bfloat16))


def twiddle_tables(wide, narrow):
    outer_idx = jnp.arange(wide, dtype=jnp.int32)
    inner_idx = jnp.arange(narrow, dtype=jnp.int32)
    phase_int = outer_idx[:, None] * inner_idx[None, :] % (wide * narrow)
    radians = phase_int.astype(jnp.float32) * (2.0 * math.pi / (wide * narrow))
    return (jnp.cos(radians)[None], jnp.sin(radians)[None])


def mix_form(form, left_op, right_op):
    return jnp.einsum(form, left_op.astype(jnp.float32), right_op.astype(jnp.float32))


def forward_local(values, tables):
    cos_w, sin_w, cos_a, sin_a = tables
    rows_all, length_dft = values.shape
    wide = cos_w.shape[0]
    narrow = length_dft // wide
    grid = values.reshape(rows_all, wide, narrow)
    section_re = mix_form("rba,bk->rka", grid, cos_w)
    section_im = -mix_form("rba,bk->rka", grid, sin_w)
    twid_cos, twid_sin = twiddle_tables(wide, narrow)
    inner_re = (section_re * twid_cos + section_im * twid_sin).astype(jnp.bfloat16)
    inner_im = (section_im * twid_cos - section_re * twid_sin).astype(jnp.bfloat16)
    out_re = mix_form("rka,ad->rdk", inner_re, cos_a) + mix_form("rka,ad->rdk", inner_im, sin_a)
    out_im = mix_form("rka,ad->rdk", inner_im, cos_a) - mix_form("rka,ad->rdk", inner_re, sin_a)
    return (out_re.reshape(rows_all, length_dft), out_im.reshape(rows_all, length_dft))


def inverse_local(values_re, values_im, tables):
    cos_w, sin_w, cos_a, sin_a = tables
    rows_all, length_dft = values_re.shape
    wide = cos_w.shape[0]
    narrow = length_dft // wide
    grid_re = values_re.reshape(rows_all, narrow, wide)
    grid_im = values_im.reshape(rows_all, narrow, wide)
    back_re = mix_form("rdk,da->rka", grid_re, cos_a) - mix_form("rdk,da->rka", grid_im, sin_a)
    back_im = mix_form("rdk,da->rka", grid_im, cos_a) + mix_form("rdk,da->rka", grid_re, sin_a)
    twid_cos, twid_sin = twiddle_tables(wide, narrow)
    outer_re = (back_re * twid_cos - back_im * twid_sin).astype(jnp.bfloat16)
    outer_im = (back_im * twid_cos + back_re * twid_sin).astype(jnp.bfloat16)
    real_part = mix_form("rka,kb->rba", outer_re, cos_w) - mix_form("rka,kb->rba", outer_im, sin_w)
    return real_part.reshape(rows_all, length_dft)


def small_mix(table, values):
    return jnp.einsum("gp,cpr->cgr", table.astype(jnp.float32), values.astype(jnp.float32))


def spectral(normed, spectrum, tables, cos_p, sin_p, send_out, send_back):
    col_width, tok_rows = normed.shape
    groups = cos_p.shape[0]
    share = tok_rows // groups
    length_all = tok_rows * groups
    device_pos = lax.axis_index("seq")
    frequency = jnp.arange(tok_rows, dtype=jnp.int32)
    radians = (frequency * device_pos).astype(jnp.float32) * (2.0 * math.pi / length_all)
    twist_cos = jnp.cos(radians)[None, :]
    twist_sin = jnp.sin(radians)[None, :]
    first_re, first_im = forward_local(normed, tables)
    twisted_re = (first_re * twist_cos + first_im * twist_sin).astype(jnp.bfloat16)
    twisted_im = (first_im * twist_cos - first_re * twist_sin).astype(jnp.bfloat16)
    moved_re, moved_im = send_out((twisted_re, twisted_im))
    moved_re = moved_re.reshape(col_width, groups, share)
    moved_im = moved_im.reshape(col_width, groups, share)
    spec_re = small_mix(cos_p, moved_re) + small_mix(sin_p, moved_im)
    spec_im = small_mix(cos_p, moved_im) - small_mix(sin_p, moved_re)
    filter_re = spectrum[0].reshape(col_width, groups, share)
    filter_im = spectrum[1].reshape(col_width, groups, share)
    filtered_re = (filter_re * spec_re - filter_im * spec_im).astype(jnp.bfloat16)
    filtered_im = (filter_re * spec_im + filter_im * spec_re).astype(jnp.bfloat16)
    back_re = small_mix(cos_p, filtered_re) - small_mix(sin_p, filtered_im)
    back_im = small_mix(cos_p, filtered_im) + small_mix(sin_p, filtered_re)
    owned_freq = device_pos * share + jnp.arange(share, dtype=jnp.int32)
    devices = jnp.arange(groups, dtype=jnp.int32)
    undo_radians = (devices[:, None] * owned_freq[None, :]).astype(jnp.float32) * (
        2.0 * math.pi / length_all
    )
    undo_cos = jnp.cos(undo_radians)[None]
    undo_sin = jnp.sin(undo_radians)[None]
    turned_re = (
        (back_re * undo_cos - back_im * undo_sin).astype(jnp.bfloat16).reshape(col_width, tok_rows)
    )
    turned_im = (
        (back_im * undo_cos + back_re * undo_sin).astype(jnp.bfloat16).reshape(col_width, tok_rows)
    )
    home_re, home_im = send_back((turned_re, turned_im))
    return inverse_local(home_re, home_im, tables) * (1.0 / length_all)


MESH = pl.DeviceIdType.MESH
VMEM_BYTES = 56 * 1024 * 1024


def vmem_spec():
    return pl.BlockSpec(memory_space=pltpu.VMEM)


def column_of(row_ref):
    size = row_ref.shape[1]
    shape = (size, size)
    on = lax.broadcasted_iota(jnp.int32, shape, 0) == lax.broadcasted_iota(jnp.int32, shape, 1)
    return jnp.sum(jnp.where(on, row_ref[...], 0.0), axis=1, keepdims=True)


def unfold(flat_ref, wide, out_ref):
    rows, cols = out_ref.shape
    pack = 1 if cols % 128 == 0 else 2
    batch = 8 // pack

    def step(i, carry):
        low = pl.multiple_of(i * (8 * cols), 128)
        for j in range(batch):
            run = flat_ref[0:1, pl.ds(low + j * pack * cols, pack * cols)].astype(jnp.float32)
            for m in range(pack):
                wide[pl.ds(i * 8 + j * pack + m, 1), 0:cols] = run[:, m * cols : (m + 1) * cols]
        return carry

    lax.fori_loop(0, rows // 8, step, 0)
    out_ref[...] = wide[0:rows, 0:cols].astype(jnp.bfloat16)


def greet(axis, n):
    me = lax.axis_index(axis)
    barrier = pltpu.get_barrier_semaphore()
    for k in range(1, n):
        pl.semaphore_signal(
            barrier, inc=1, device_id={axis: lax.rem(me + k, n)}, device_id_type=MESH
        )
    return barrier


def share_stats(n, stats, send_sem, recv_sem):
    me = lax.axis_index("chan")
    copies = []
    for k in range(1, n):
        copy = pltpu.make_async_remote_copy(
            src_ref=stats.at[0],
            dst_ref=stats.at[k],
            send_sem=send_sem.at[k],
            recv_sem=recv_sem.at[k],
            device_id={"chan": lax.rem(me + k, n)},
            device_id_type=MESH,
        )
        copy.start()
        copies.append(copy)
    for copy in copies:
        copy.wait()
    total = stats[0]
    for k in range(1, n):
        total = total + stats[k]
    return total


def norm_kernel(n, width, x_ref, gain_ref, out_ref, stats, send_sem, recv_sem):
    barrier = greet("chan", n)
    norm_body(n, width, barrier, n - 1, x_ref, gain_ref, out_ref, stats, send_sem, recv_sem)


def norm_body(n, width, barrier, signals, x_ref, gain_ref, out_ref, stats, send_sem, recv_sem):
    cols = x_ref.shape[1]
    step = min(cols, 512)
    for c in range(0, cols, step):
        x = x_ref[:, c : c + step].astype(jnp.float32)
        stats[0, 0:1, c : c + step] = jnp.sum(x, axis=0, keepdims=True)
        stats[0, 1:2, c : c + step] = jnp.sum(x * x, axis=0, keepdims=True)
    pl.semaphore_wait(barrier, signals)
    total = share_stats(n, stats, send_sem, recv_sem)
    mean = total[0:1] / width
    scale = lax.rsqrt(total[1:2] / width - mean * mean + 1e-05)
    gain = column_of(gain_ref)
    for c in range(0, cols, step):
        x = x_ref[:, c : c + step].astype(jnp.float32)
        y = (x - mean[:, c : c + step]) * scale[:, c : c + step] * gain
        out_ref[:, c : c + step] = y.astype(jnp.bfloat16)


def first_norm(n, width, tokens, gain):
    return pl.pallas_call(
        functools.partial(norm_kernel, n, width),
        out_shape=jax.ShapeDtypeStruct(tokens.shape, jnp.bfloat16),
        in_specs=[vmem_spec()] * 2,
        out_specs=vmem_spec(),
        scratch_shapes=[
            pltpu.VMEM((n, 2, tokens.shape[1]), jnp.float32),
            pltpu.SemaphoreType.DMA((n,)),
            pltpu.SemaphoreType.DMA((n,)),
        ],
        compiler_params=pltpu.CompilerParams(
            collective_id=0, has_side_effects=True, vmem_limit_bytes=VMEM_BYTES
        ),
    )(tokens, gain[None])


def small_dft(values, sign):
    n = len(values)
    if n == 1:
        return values
    even = small_dft(values[0::2], sign)
    odd = small_dft(values[1::2], sign)
    out = [None] * n
    for k in range(n // 2):
        re, im = odd[k]
        if k == 0:
            tr, ti = re, im
        elif 4 * k == n:
            tr, ti = (-im, re) if sign > 0 else (im, -re)
        else:
            c = float(np.float64(math.cos(2 * math.pi * k / n)).astype(jnp.bfloat16))
            s = sign * float(np.float64(math.sin(2 * math.pi * k / n)).astype(jnp.bfloat16))
            tr, ti = re * c - im * s, re * s + im * c
        er, ei = even[k]
        out[k] = (er + tr, ei + ti)
        out[k + n // 2] = (er - tr, ei - ti)
    return out


def conv_kernel(
    n, n_chan, width, tok_ref, gain_ref, filt_hbm, cos_hbm, sin_hbm,
    twc_ref, tws_ref, undo_c, undo_s,
    mi_flat, up_flat, down_flat, mo_flat,
    out_ref, x_ref, mi_ref, up_ref, down_ref, mo_ref, wide,
    cos_v, sin_v, filt_v, send_f, recv_f, send_b, recv_b, stats,
    st_send, st_recv, load_sem, filt_sem, sf_sem, rf_sem, sb_sem, rb_sem,
):
    me = lax.axis_index("seq")
    barrier = greet("seq", n)
    greet("chan", n_chan)
    rows, cols = x_ref.shape
    share = cols // n
    parts = sf_sem.shape[1]
    group = rows // parts
    pieces = sb_sem.shape[1]
    piece = rows // pieces

    def block_of(k):
        return pl.ds(pl.multiple_of(lax.rem(me + k, n) * share, share), share)

    def load(k, which):
        hbm, vmem = ((cos_hbm, cos_v), (sin_hbm, sin_v))[which]
        view = block_of(k)
        return pltpu.make_async_copy(hbm.at[:, view], vmem.at[:, view], load_sem.at[k, which])

    filt_copy = pltpu.make_async_copy(filt_hbm, filt_v, filt_sem.at[0])
    for k in list(range(1, n)) + [0]:
        load(k, 0).start()
        load(k, 1).start()
    filt_copy.start()
    norm_body(
        n_chan, width, barrier, n + n_chan - 2, tok_ref, gain_ref, x_ref, stats, st_send, st_recv
    )

    def transform(k, part):
        if part == 0:
            load(k, 0).wait()
            load(k, 1).wait()
        view = block_of(k)
        x = x_ref[part * group : (part + 1) * group, :]
        re = jnp.dot(x, cos_v[:, view], preferred_element_type=jnp.float32)
        im = -jnp.dot(x, sin_v[:, view], preferred_element_type=jnp.float32)
        tc, ts = twc_ref[me, :, view], tws_ref[me, :, view]
        return (
            (re * tc + im * ts).astype(jnp.bfloat16),
            (im * tc - re * ts).astype(jnp.bfloat16),
        )

    def rows_of(part):
        return pl.ds(part * group, group)

    def outward(k, part):
        return pltpu.make_async_remote_copy(
            src_ref=send_f.at[k, :, rows_of(part)],
            dst_ref=recv_f.at[me, :, rows_of(part)],
            send_sem=sf_sem.at[k, part],
            recv_sem=rf_sem.at[k, part],
            device_id={"seq": lax.rem(me + k, n)},
            device_id_type=MESH,
        )

    for part in range(parts):

        def forward(k, carry, part=part):
            re, im = transform(k, part)
            send_f[k, 0, rows_of(part)] = re
            send_f[k, 1, rows_of(part)] = im
            outward(k, part).start()
            return carry

        lax.fori_loop(1, n, forward, 0)
        re, im = transform(0, part)
        recv_f[me, 0, rows_of(part)] = re
        recv_f[me, 1, rows_of(part)] = im
    filt_copy.wait()

    def inward(k, part):
        peer = lax.rem(me + k, n)
        view = pl.ds(part * piece, piece)
        return pltpu.make_async_remote_copy(
            src_ref=send_b.at[peer, :, view],
            dst_ref=recv_b.at[k, :, view],
            send_sem=sb_sem.at[k, part],
            recv_sem=rb_sem.at[k, part],
            device_id={"seq": peer},
            device_id_type=MESH,
        )

    lanes = 128
    for flat, square in (
        (mi_flat, mi_ref), (up_flat, up_ref), (down_flat, down_ref), (mo_flat, mo_ref)
    ):
        unfold(flat, wide, square)

    for part in range(parts):

        def arrive(k, carry, part=part):
            outward(k, part).wait()
            return carry

        lax.fori_loop(1, n, arrive, 0)

    for part in range(pieces):

        def middle(i, carry, part=part):
            view = pl.ds(pl.multiple_of(part * piece + i * 16, 16), 16)
            for c in range(0, share, lanes):
                values = [
                    (
                        recv_f[p, 0, view, c : c + lanes].astype(jnp.float32),
                        recv_f[p, 1, view, c : c + lanes].astype(jnp.float32),
                    )
                    for p in range(n)
                ]
                spec = small_dft(values, -1)
                filtered = []
                for g in range(n):
                    sr, si = spec[g]
                    low = g * share + c
                    fr = filt_v[0, view, low : low + lanes]
                    fi = filt_v[1, view, low : low + lanes]
                    filtered.append((fr * sr - fi * si, fr * si + fi * sr))
                back = small_dft(filtered, 1)
                for p in range(n):
                    br, bi = back[p]
                    uc = undo_c[me, p : p + 1, c : c + lanes]
                    us = undo_s[me, p : p + 1, c : c + lanes]
                    send_b[p, 0, view, c : c + lanes] = (br * uc - bi * us).astype(jnp.bfloat16)
                    send_b[p, 1, view, c : c + lanes] = (bi * uc + br * us).astype(jnp.bfloat16)
            return carry

        lax.fori_loop(0, piece // 16, middle, 0)

        def push(k, carry, part=part):
            inward(k, part).start()
            return carry

        lax.fori_loop(1, n, push, 0)

    tile = min(cols, 512)
    scale = 1.0 / (n * cols)

    def accumulate(re, im, source, part, first):
        view = pl.ds(pl.multiple_of(source * share, share), share)

        def column(t, carry):
            low = pl.ds(pl.multiple_of(t * tile, tile), tile)
            term = jnp.dot(re, cos_v[view, low], preferred_element_type=jnp.float32) - jnp.dot(
                im, sin_v[view, low], preferred_element_type=jnp.float32
            )
            if first:
                out_ref[rows_of(part), low] = term * scale
            else:
                out_ref[rows_of(part), low] += term * scale
            return carry

        lax.fori_loop(0, cols // tile, column, 0)

    for part in range(parts):
        accumulate(send_b[me, 0, rows_of(part)], send_b[me, 1, rows_of(part)], me, part, True)
    for part in range(parts):

        def back_step(k, carry, part=part):
            for sub in range(pieces // parts):
                inward(k, part * (pieces // parts) + sub).wait()
            source = lax.rem(me + n - k, n)
            accumulate(
                recv_b[k, 0, rows_of(part)], recv_b[k, 1, rows_of(part)], source, part, False
            )
            return carry

        lax.fori_loop(1, n, back_step, 0)


def convolve_kernel(n, n_chan, width, tokens, gain, spectrum, flats):
    rows, cols = tokens.shape
    hidden = flats[1].shape[1] // rows
    shapes = [(rows, cols), (rows, rows), (rows, hidden), (hidden, rows), (rows, rows)]
    share = cols // n
    index = np.arange(cols)
    angle = (index[:, None] * index[None, :] % cols) * (2.0 * math.pi / cols)
    cos_m = jnp.asarray(np.cos(angle).astype(jnp.bfloat16))
    sin_m = jnp.asarray(np.sin(angle).astype(jnp.bfloat16))
    turn = 2.0 * math.pi / (n * cols)
    ranks = np.arange(n)
    twist = ranks[:, None, None] * index[None, None, :] * turn
    owned = ranks[:, None] * share + np.arange(share)[None]
    undo = ranks[None, :, None] * owned[:, None, :] * turn
    small = [
        jnp.asarray(form(angles).astype(np.float32))
        for angles in (twist, undo)
        for form in (np.cos, np.sin)
    ]
    pieces = 4 if rows % 64 == 0 else 1
    block = pltpu.VMEM((n, 2, rows, share), jnp.bfloat16)
    dma = pltpu.SemaphoreType.DMA
    whole, cut = dma((n, 1)), dma((n, pieces))
    return pl.pallas_call(
        functools.partial(conv_kernel, n, n_chan, width),
        out_shape=[jax.ShapeDtypeStruct((rows, cols), jnp.float32)]
        + [jax.ShapeDtypeStruct(shape, jnp.bfloat16) for shape in shapes],
        in_specs=[vmem_spec()] * 2 + [pl.BlockSpec(memory_space=pl.ANY)] * 3 + [vmem_spec()] * 8,
        out_specs=[vmem_spec()] * 6,
        scratch_shapes=[
            pltpu.VMEM((max(rows, hidden),) * 2, jnp.float32),
            pltpu.VMEM((cols, cols), jnp.bfloat16),
            pltpu.VMEM((cols, cols), jnp.bfloat16),
            pltpu.VMEM(spectrum.shape, jnp.float32),
            block, block, block, block,
            pltpu.VMEM((n_chan, 2, cols), jnp.float32),
            dma((n_chan,)), dma((n_chan,)), dma((n, 2)), dma((1,)), whole, whole, cut, cut,
        ],
        compiler_params=pltpu.CompilerParams(
            collective_id=1, has_side_effects=True, vmem_limit_bytes=VMEM_BYTES
        ),
    )(tokens, gain[None], spectrum, cos_m, sin_m, *small, *flats)


def across(left, right):
    return lax.dot_general(
        left, right, (((0,), (0,)), ((), ())), preferred_element_type=jnp.float32
    )


def mlp_kernel(
    n, width, tok_ref, conv_ref, norm_ref, skip_ref, gain_ref, mi_ref, up_ref, down_ref, mo_ref,
    out_ref, resid, stats, first, regrouped, lowered, returned,
    st_send, st_recv, send_sem, recv_sem,
):
    me = lax.axis_index("chan")
    barrier = greet("chan", n)
    rows, cols = tok_ref.shape
    chunks, _, step = first.shape
    piece = rows // n
    skip, gain = column_of(skip_ref), column_of(gain_ref)

    def residual_of(c, carry):
        view = pl.ds(pl.multiple_of(c * step, step), step)
        value = (
            tok_ref[:, view].astype(jnp.float32)
            + conv_ref[:, view]
            + skip * norm_ref[:, view].astype(jnp.float32)
        ).astype(jnp.bfloat16)
        resid[:, view] = value
        value = value.astype(jnp.float32)
        stats[0, 0:1, view] = jnp.sum(value, axis=0, keepdims=True)
        stats[0, 1:2, view] = jnp.sum(value * value, axis=0, keepdims=True)
        return carry

    lax.fori_loop(0, chunks, residual_of, 0)
    pl.semaphore_wait(barrier, n - 1)
    total = share_stats(n, stats, st_send, st_recv)
    mean = total[0:1] / width
    stats[0, 0:1, :] = mean
    stats[0, 1:2, :] = lax.rsqrt(total[1:2] / width - mean * mean + 1e-05)

    def exchange(phase, c, k):
        peer = lax.rem(me + k, n)
        source, target = ((first, regrouped), (lowered, returned))[phase]
        return pltpu.make_async_remote_copy(
            src_ref=source.at[c, pl.ds(pl.multiple_of(peer * piece, 16), piece)],
            dst_ref=target.at[c, pl.ds(pl.multiple_of(me * piece, 16), piece)],
            send_sem=send_sem.at[phase, c, k],
            recv_sem=recv_sem.at[phase, c, k],
            device_id={"chan": peer},
            device_id_type=MESH,
        )

    own = pl.ds(pl.multiple_of(me * piece, 16), piece)

    def first_step(c, carry):
        view = pl.ds(pl.multiple_of(c * step, step), step)
        value = resid[:, view].astype(jnp.float32)
        value = (value - stats[0, 0:1, view]) * stats[0, 1:2, view] * gain
        first[c] = across(mi_ref[...], value.astype(jnp.bfloat16)).astype(jnp.bfloat16)
        for k in range(1, n):
            exchange(0, c, k).start()
        regrouped[c, own] = first[c, own]
        return carry

    lax.fori_loop(0, chunks, first_step, 0)

    def second_step(c, carry):
        for k in range(1, n):
            exchange(0, c, k).wait()
        pre = across(up_ref[...], regrouped[c])
        hidden = 0.5 * pre * (1.0 + lax.erf(pre * math.sqrt(0.5)))
        lowered[c] = across(down_ref[...], hidden.astype(jnp.bfloat16)).astype(jnp.bfloat16)
        for k in range(1, n):
            exchange(1, c, k).start()
        returned[c, own] = lowered[c, own]
        return carry

    lax.fori_loop(0, chunks, second_step, 0)

    def third_step(c, carry):
        view = pl.ds(pl.multiple_of(c * step, step), step)
        for k in range(1, n):
            exchange(1, c, k).wait()
        term = across(mo_ref[...], returned[c])
        out_ref[:, view] = (resid[:, view].astype(jnp.float32) + term).astype(jnp.bfloat16)
        return carry

    lax.fori_loop(0, chunks, third_step, 0)


def mlp(n, width, *operands):
    rows, cols = operands[0].shape
    step = 256 if cols % 256 == 0 else cols
    chunks = cols // step
    block = pltpu.VMEM((chunks, rows, step), jnp.bfloat16)
    dma = pltpu.SemaphoreType.DMA
    return pl.pallas_call(
        functools.partial(mlp_kernel, n, width),
        out_shape=jax.ShapeDtypeStruct((rows, cols), jnp.bfloat16),
        in_specs=[vmem_spec()] * len(operands),
        out_specs=vmem_spec(),
        scratch_shapes=[
            pltpu.VMEM((rows, cols), jnp.bfloat16),
            pltpu.VMEM((n, 2, cols), jnp.float32),
            block, block, block, block,
            dma((n,)), dma((n,)), dma((2, chunks, n)), dma((2, chunks, n)),
        ],
        compiler_params=pltpu.CompilerParams(
            collective_id=2, has_side_effects=True, vmem_limit_bytes=VMEM_BYTES
        ),
    )(*operands)


def shards(
    tokens,
    filter_spectrum,
    skip_weight,
    norm_gain,
    mlp_gain,
    mix_in,
    up_weight,
    down_weight,
    mix_out,
):
    columns, tok_rows = tokens.shape
    groups = lax.axis_size("seq")
    blocks = lax.axis_size("chan")
    width = columns * blocks
    hidden_width = up_weight.shape[1] // columns
    flats = (mix_in, up_weight, down_weight, mix_out)
    if groups == 8 and (tok_rows // groups) % 128 == 0:
        convolved, normed, *factors = convolve_kernel(
            groups, blocks, width, tokens, norm_gain, filter_spectrum, flats
        )
    else:
        normed = first_norm(blocks, width, tokens, norm_gain)
        cos_w, sin_w = dft_tables(RADIX)
        cos_a, sin_a = dft_tables(tok_rows // RADIX)
        cos_p, sin_p = dft_tables(groups)

        def swap(pair_in):
            return tuple(
                lax.all_to_all(half, "seq", split_axis=1, concat_axis=1, tiled=True)
                for half in pair_in
            )

        convolved = spectral(
            normed, filter_spectrum, (cos_w, sin_w, cos_a, sin_a), cos_p, sin_p, swap, swap
        )
        shapes = ((columns, columns), (columns, hidden_width), (hidden_width, columns))
        factors = [flat.reshape(shape) for flat, shape in zip(flats, shapes + shapes[:1])]
    return mlp(
        blocks,
        width,
        tokens,
        convolved,
        normed,
        skip_weight[None],
        mlp_gain[None],
        *factors,
    )


def solution(mesh):
    in_specs = (
        P("chan", "seq"),
        P(None, "chan", "seq"),
        P("chan"),
        P("chan"),
        P("chan"),
        P("chan", None),
        P("chan", None),
        P("chan", None),
        P("chan", None),
    )
    out_specs = P("chan", "seq")
    return jax.shard_map(shards, mesh=mesh, in_specs=in_specs, out_specs=out_specs, check_vma=False)
```

```python
import functools
import math

import jax
import jax.numpy as jnp
import numpy as np
from jax import lax
from jax.experimental import pallas as pl
from jax.experimental.pallas import tpu as pltpu
from jax.sharding import PartitionSpec as P

RADIX = 64


def dft_tables(length_dft):
    position = jnp.arange(length_dft, dtype=jnp.int32)
    phase_int = position[:, None] * position[None, :] % length_dft
    radians = phase_int.astype(jnp.float32) * (2.0 * math.pi / length_dft)
    return (jnp.cos(radians).astype(jnp.bfloat16), jnp.sin(radians).astype(jnp.bfloat16))


def twiddle_tables(wide, narrow):
    outer_idx = jnp.arange(wide, dtype=jnp.int32)
    inner_idx = jnp.arange(narrow, dtype=jnp.int32)
    phase_int = outer_idx[:, None] * inner_idx[None, :] % (wide * narrow)
    radians = phase_int.astype(jnp.float32) * (2.0 * math.pi / (wide * narrow))
    return (jnp.cos(radians)[None], jnp.sin(radians)[None])


def mix_form(form, left_op, right_op):
    return jnp.einsum(form, left_op.astype(jnp.float32), right_op.astype(jnp.float32))


def forward_local(values, tables):
    cos_w, sin_w, cos_a, sin_a = tables
    rows_all, length_dft = values.shape
    wide = cos_w.shape[0]
    narrow = length_dft // wide
    grid = values.reshape(rows_all, wide, narrow)
    section_re = mix_form("rba,bk->rka", grid, cos_w)
    section_im = -mix_form("rba,bk->rka", grid, sin_w)
    twid_cos, twid_sin = twiddle_tables(wide, narrow)
    inner_re = (section_re * twid_cos + section_im * twid_sin).astype(jnp.bfloat16)
    inner_im = (section_im * twid_cos - section_re * twid_sin).astype(jnp.bfloat16)
    out_re = mix_form("rka,ad->rdk", inner_re, cos_a) + mix_form("rka,ad->rdk", inner_im, sin_a)
    out_im = mix_form("rka,ad->rdk", inner_im, cos_a) - mix_form("rka,ad->rdk", inner_re, sin_a)
    return (out_re.reshape(rows_all, length_dft), out_im.reshape(rows_all, length_dft))


def inverse_local(values_re, values_im, tables):
    cos_w, sin_w, cos_a, sin_a = tables
    rows_all, length_dft = values_re.shape
    wide = cos_w.shape[0]
    narrow = length_dft // wide
    grid_re = values_re.reshape(rows_all, narrow, wide)
    grid_im = values_im.reshape(rows_all, narrow, wide)
    back_re = mix_form("rdk,da->rka", grid_re, cos_a) - mix_form("rdk,da->rka", grid_im, sin_a)
    back_im = mix_form("rdk,da->rka", grid_im, cos_a) + mix_form("rdk,da->rka", grid_re, sin_a)
    twid_cos, twid_sin = twiddle_tables(wide, narrow)
    outer_re = (back_re * twid_cos - back_im * twid_sin).astype(jnp.bfloat16)
    outer_im = (back_im * twid_cos + back_re * twid_sin).astype(jnp.bfloat16)
    real_part = mix_form("rka,kb->rba", outer_re, cos_w) - mix_form("rka,kb->rba", outer_im, sin_w)
    return real_part.reshape(rows_all, length_dft)


def small_mix(table, values):
    return jnp.einsum("gp,cpr->cgr", table.astype(jnp.float32), values.astype(jnp.float32))


def spectral(normed, spectrum, tables, cos_p, sin_p, send_out, send_back):
    col_width, tok_rows = normed.shape
    groups = cos_p.shape[0]
    share = tok_rows // groups
    length_all = tok_rows * groups
    device_pos = lax.axis_index("seq")
    frequency = jnp.arange(tok_rows, dtype=jnp.int32)
    radians = (frequency * device_pos).astype(jnp.float32) * (2.0 * math.pi / length_all)
    twist_cos = jnp.cos(radians)[None, :]
    twist_sin = jnp.sin(radians)[None, :]
    first_re, first_im = forward_local(normed, tables)
    twisted_re = (first_re * twist_cos + first_im * twist_sin).astype(jnp.bfloat16)
    twisted_im = (first_im * twist_cos - first_re * twist_sin).astype(jnp.bfloat16)
    moved_re, moved_im = send_out((twisted_re, twisted_im))
    moved_re = moved_re.reshape(col_width, groups, share)
    moved_im = moved_im.reshape(col_width, groups, share)
    spec_re = small_mix(cos_p, moved_re) + small_mix(sin_p, moved_im)
    spec_im = small_mix(cos_p, moved_im) - small_mix(sin_p, moved_re)
    filter_re = spectrum[0].reshape(col_width, groups, share)
    filter_im = spectrum[1].reshape(col_width, groups, share)
    filtered_re = (filter_re * spec_re - filter_im * spec_im).astype(jnp.bfloat16)
    filtered_im = (filter_re * spec_im + filter_im * spec_re).astype(jnp.bfloat16)
    back_re = small_mix(cos_p, filtered_re) - small_mix(sin_p, filtered_im)
    back_im = small_mix(cos_p, filtered_im) + small_mix(sin_p, filtered_re)
    owned_freq = device_pos * share + jnp.arange(share, dtype=jnp.int32)
    devices = jnp.arange(groups, dtype=jnp.int32)
    undo_radians = (devices[:, None] * owned_freq[None, :]).astype(jnp.float32) * (
        2.0 * math.pi / length_all
    )
    undo_cos = jnp.cos(undo_radians)[None]
    undo_sin = jnp.sin(undo_radians)[None]
    turned_re = (
        (back_re * undo_cos - back_im * undo_sin).astype(jnp.bfloat16).reshape(col_width, tok_rows)
    )
    turned_im = (
        (back_im * undo_cos + back_re * undo_sin).astype(jnp.bfloat16).reshape(col_width, tok_rows)
    )
    home_re, home_im = send_back((turned_re, turned_im))
    return inverse_local(home_re, home_im, tables) * (1.0 / length_all)


MESH = pl.DeviceIdType.MESH
VMEM_BYTES = 56 * 1024 * 1024


def vmem_spec():
    return pl.BlockSpec(memory_space=pltpu.VMEM)


def column_of(row_ref):
    size = row_ref.shape[1]
    shape = (size, size)
    on = lax.broadcasted_iota(jnp.int32, shape, 0) == lax.broadcasted_iota(jnp.int32, shape, 1)
    return jnp.sum(jnp.where(on, row_ref[...], 0.0), axis=1, keepdims=True)


def unfold(flat_ref, wide, out_ref):
    rows, cols = out_ref.shape
    pack = 1 if cols % 128 == 0 else 2
    batch = 8 // pack

    def step(i, carry):
        low = pl.multiple_of(i * (8 * cols), 128)
        for j in range(batch):
            run = flat_ref[0:1, pl.ds(low + j * pack * cols, pack * cols)].astype(jnp.float32)
            for m in range(pack):
                wide[pl.ds(i * 8 + j * pack + m, 1), 0:cols] = run[:, m * cols : (m + 1) * cols]
        return carry

    lax.fori_loop(0, rows // 8, step, 0)
    out_ref[...] = wide[0:rows, 0:cols].astype(jnp.bfloat16)


def greet(axis, n):
    me = lax.axis_index(axis)
    barrier = pltpu.get_barrier_semaphore()
    for k in range(1, n):
        pl.semaphore_signal(
            barrier, inc=1, device_id={axis: lax.rem(me + k, n)}, device_id_type=MESH
        )
    return barrier


def share_stats(n, stats, send_sem, recv_sem):
    me = lax.axis_index("chan")
    copies = []
    for k in range(1, n):
        copy = pltpu.make_async_remote_copy(
            src_ref=stats.at[0],
            dst_ref=stats.at[k],
            send_sem=send_sem.at[k],
            recv_sem=recv_sem.at[k],
            device_id={"chan": lax.rem(me + k, n)},
            device_id_type=MESH,
        )
        copy.start()
        copies.append(copy)
    for copy in copies:
        copy.wait()
    total = stats[0]
    for k in range(1, n):
        total = total + stats[k]
    return total


def norm_kernel(n, width, x_ref, gain_ref, out_ref, stats, send_sem, recv_sem):
    barrier = greet("chan", n)
    norm_body(n, width, barrier, n - 1, x_ref, gain_ref, out_ref, stats, send_sem, recv_sem)


def norm_body(n, width, barrier, signals, x_ref, gain_ref, out_ref, stats, send_sem, recv_sem):
    cols = x_ref.shape[1]
    step = min(cols, 512)
    for c in range(0, cols, step):
        x = x_ref[:, c : c + step].astype(jnp.float32)
        stats[0, 0:1, c : c + step] = jnp.sum(x, axis=0, keepdims=True)
        stats[0, 1:2, c : c + step] = jnp.sum(x * x, axis=0, keepdims=True)
    pl.semaphore_wait(barrier, signals)
    total = share_stats(n, stats, send_sem, recv_sem)
    mean = total[0:1] / width
    scale = lax.rsqrt(total[1:2] / width - mean * mean + 1e-05)
    gain = column_of(gain_ref)
    for c in range(0, cols, step):
        x = x_ref[:, c : c + step].astype(jnp.float32)
        y = (x - mean[:, c : c + step]) * scale[:, c : c + step] * gain
        out_ref[:, c : c + step] = y.astype(jnp.bfloat16)


def first_norm(n, width, tokens, gain):
    return pl.pallas_call(
        functools.partial(norm_kernel, n, width),
        out_shape=jax.ShapeDtypeStruct(tokens.shape, jnp.bfloat16),
        in_specs=[vmem_spec()] * 2,
        out_specs=vmem_spec(),
        scratch_shapes=[
            pltpu.VMEM((n, 2, tokens.shape[1]), jnp.float32),
            pltpu.SemaphoreType.DMA((n,)),
            pltpu.SemaphoreType.DMA((n,)),
        ],
        compiler_params=pltpu.CompilerParams(
            collective_id=0, has_side_effects=True, vmem_limit_bytes=VMEM_BYTES
        ),
    )(tokens, gain[None])


def small_dft(values, sign):
    n = len(values)
    if n == 1:
        return values
    even = small_dft(values[0::2], sign)
    odd = small_dft(values[1::2], sign)
    out = [None] * n
    for k in range(n // 2):
        re, im = odd[k]
        if k == 0:
            tr, ti = re, im
        elif 4 * k == n:
            tr, ti = (-im, re) if sign > 0 else (im, -re)
        else:
            c = float(np.float64(math.cos(2 * math.pi * k / n)).astype(jnp.bfloat16))
            s = sign * float(np.float64(math.sin(2 * math.pi * k / n)).astype(jnp.bfloat16))
            tr, ti = re * c - im * s, re * s + im * c
        er, ei = even[k]
        out[k] = (er + tr, ei + ti)
        out[k + n // 2] = (er - tr, ei - ti)
    return out


def conv_kernel(
    n, n_chan, width, tok_ref, gain_ref, filt_hbm, cos_hbm, sin_hbm,
    twc_ref, tws_ref, undo_c, undo_s,
    mi_flat, up_flat, down_flat, mo_flat,
    out_ref, x_ref, mi_ref, up_ref, down_ref, mo_ref, wide,
    cos_v, sin_v, filt_v, send_f, recv_f, send_b, recv_b, stats,
    st_send, st_recv, load_sem, filt_sem, sf_sem, rf_sem, sb_sem, rb_sem,
):
    me = lax.axis_index("seq")
    barrier = greet("seq", n)
    greet("chan", n_chan)
    rows, cols = x_ref.shape
    share = cols // n
    parts = sf_sem.shape[1]
    group = rows // parts
    pieces = sb_sem.shape[1]
    piece = rows // pieces

    def block_of(k):
        return pl.ds(pl.multiple_of(lax.rem(me + k, n) * share, share), share)

    def load(k, which):
        hbm, vmem = ((cos_hbm, cos_v), (sin_hbm, sin_v))[which]
        view = block_of(k)
        return pltpu.make_async_copy(hbm.at[:, view], vmem.at[:, view], load_sem.at[k, which])

    filt_copy = pltpu.make_async_copy(filt_hbm, filt_v, filt_sem.at[0])
    for k in list(range(1, n)) + [0]:
        load(k, 0).start()
        load(k, 1).start()
    filt_copy.start()
    norm_body(
        n_chan, width, barrier, n + n_chan - 2, tok_ref, gain_ref, x_ref, stats, st_send, st_recv
    )

    def transform(k, part):
        if part == 0:
            load(k, 0).wait()
            load(k, 1).wait()
        view = block_of(k)
        x = x_ref[part * group : (part + 1) * group, :]
        re = jnp.dot(x, cos_v[:, view], preferred_element_type=jnp.float32)
        im = -jnp.dot(x, sin_v[:, view], preferred_element_type=jnp.float32)
        tc, ts = twc_ref[me, :, view], tws_ref[me, :, view]
        return (
            (re * tc + im * ts).astype(jnp.bfloat16),
            (im * tc - re * ts).astype(jnp.bfloat16),
        )

    def rows_of(part):
        return pl.ds(part * group, group)

    def outward(k, part):
        return pltpu.make_async_remote_copy(
            src_ref=send_f.at[k, :, rows_of(part)],
            dst_ref=recv_f.at[me, :, rows_of(part)],
            send_sem=sf_sem.at[k, part],
            recv_sem=rf_sem.at[k, part],
            device_id={"seq": lax.rem(me + k, n)},
            device_id_type=MESH,
        )

    for part in range(parts):

        def forward(k, carry, part=part):
            re, im = transform(k, part)
            send_f[k, 0, rows_of(part)] = re
            send_f[k, 1, rows_of(part)] = im
            outward(k, part).start()
            return carry

        lax.fori_loop(1, n, forward, 0)
        re, im = transform(0, part)
        recv_f[me, 0, rows_of(part)] = re
        recv_f[me, 1, rows_of(part)] = im
    filt_copy.wait()

    def inward(k, part):
        peer = lax.rem(me + k, n)
        view = pl.ds(part * piece, piece)
        return pltpu.make_async_remote_copy(
            src_ref=send_b.at[peer, :, view],
            dst_ref=recv_b.at[k, :, view],
            send_sem=sb_sem.at[k, part],
            recv_sem=rb_sem.at[k, part],
            device_id={"seq": peer},
            device_id_type=MESH,
        )

    lanes = 128
    for flat, square in (
        (mi_flat, mi_ref), (up_flat, up_ref), (down_flat, down_ref), (mo_flat, mo_ref)
    ):
        unfold(flat, wide, square)

    for part in range(parts):

        def arrive(k, carry, part=part):
            outward(k, part).wait()
            return carry

        lax.fori_loop(1, n, arrive, 0)

    for part in range(pieces):

        def middle(i, carry, part=part):
            view = pl.ds(pl.multiple_of(part * piece + i * 16, 16), 16)
            for c in range(0, share, lanes):
                values = [
                    (
                        recv_f[p, 0, view, c : c + lanes].astype(jnp.float32),
                        recv_f[p, 1, view, c : c + lanes].astype(jnp.float32),
                    )
                    for p in range(n)
                ]
                spec = small_dft(values, -1)
                filtered = []
                for g in range(n):
                    sr, si = spec[g]
                    low = g * share + c
                    fr = filt_v[0, view, low : low + lanes]
                    fi = filt_v[1, view, low : low + lanes]
                    filtered.append((fr * sr - fi * si, fr * si + fi * sr))
                back = small_dft(filtered, 1)
                for p in range(n):
                    br, bi = back[p]
                    uc = undo_c[me, p : p + 1, c : c + lanes]
                    us = undo_s[me, p : p + 1, c : c + lanes]
                    send_b[p, 0, view, c : c + lanes] = (br * uc - bi * us).astype(jnp.bfloat16)
                    send_b[p, 1, view, c : c + lanes] = (bi * uc + br * us).astype(jnp.bfloat16)
            return carry

        lax.fori_loop(0, piece // 16, middle, 0)

        def push(k, carry, part=part):
            inward(k, part).start()
            return carry

        lax.fori_loop(1, n, push, 0)

    tile = min(cols, 512)
    scale = 1.0 / (n * cols)

    def accumulate(re, im, source, part, first):
        view = pl.ds(pl.multiple_of(source * share, share), share)

        def column(t, carry):
            low = pl.ds(pl.multiple_of(t * tile, tile), tile)
            term = jnp.dot(re, cos_v[view, low], preferred_element_type=jnp.float32) - jnp.dot(
                im, sin_v[view, low], preferred_element_type=jnp.float32
            )
            if first:
                out_ref[rows_of(part), low] = term * scale
            else:
                out_ref[rows_of(part), low] += term * scale
            return carry

        lax.fori_loop(0, cols // tile, column, 0)

    for part in range(parts):
        accumulate(send_b[me, 0, rows_of(part)], send_b[me, 1, rows_of(part)], me, part, True)
    for part in range(parts):

        def back_step(k, carry, part=part):
            for sub in range(pieces // parts):
                inward(k, part * (pieces // parts) + sub).wait()
            source = lax.rem(me + n - k, n)
            accumulate(
                recv_b[k, 0, rows_of(part)], recv_b[k, 1, rows_of(part)], source, part, False
            )
            return carry

        lax.fori_loop(1, n, back_step, 0)


def convolve_kernel(n, n_chan, width, tokens, gain, spectrum, flats):
    rows, cols = tokens.shape
    hidden = flats[1].shape[1] // rows
    shapes = [(rows, cols), (rows, rows), (rows, hidden), (hidden, rows), (rows, rows)]
    share = cols // n
    index = np.arange(cols)
    angle = (index[:, None] * index[None, :] % cols) * (2.0 * math.pi / cols)
    cos_m = jnp.asarray(np.cos(angle).astype(jnp.bfloat16))
    sin_m = jnp.asarray(np.sin(angle).astype(jnp.bfloat16))
    turn = 2.0 * math.pi / (n * cols)
    ranks = np.arange(n)
    twist = ranks[:, None, None] * index[None, None, :] * turn
    owned = ranks[:, None] * share + np.arange(share)[None]
    undo = ranks[None, :, None] * owned[:, None, :] * turn
    small = [
        jnp.asarray(form(angles).astype(np.float32))
        for angles in (twist, undo)
        for form in (np.cos, np.sin)
    ]
    pieces = 4 if rows % 64 == 0 else 1
    block = pltpu.VMEM((n, 2, rows, share), jnp.bfloat16)
    dma = pltpu.SemaphoreType.DMA
    whole, cut = dma((n, 1)), dma((n, pieces))
    return pl.pallas_call(
        functools.partial(conv_kernel, n, n_chan, width),
        out_shape=[jax.ShapeDtypeStruct((rows, cols), jnp.float32)]
        + [jax.ShapeDtypeStruct(shape, jnp.bfloat16) for shape in shapes],
        in_specs=[vmem_spec()] * 2 + [pl.BlockSpec(memory_space=pl.ANY)] * 3 + [vmem_spec()] * 8,
        out_specs=[vmem_spec()] * 6,
        scratch_shapes=[
            pltpu.VMEM((max(rows, hidden),) * 2, jnp.float32),
            pltpu.VMEM((cols, cols), jnp.bfloat16),
            pltpu.VMEM((cols, cols), jnp.bfloat16),
            pltpu.VMEM(spectrum.shape, jnp.float32),
            block, block, block, block,
            pltpu.VMEM((n_chan, 2, cols), jnp.float32),
            dma((n_chan,)), dma((n_chan,)), dma((n, 2)), dma((1,)), whole, whole, cut, cut,
        ],
        compiler_params=pltpu.CompilerParams(
            collective_id=1, has_side_effects=True, vmem_limit_bytes=VMEM_BYTES
        ),
    )(tokens, gain[None], spectrum, cos_m, sin_m, *small, *flats)


def across(left, right):
    return lax.dot_general(
        left, right, (((0,), (0,)), ((), ())), preferred_element_type=jnp.float32
    )


def mlp_kernel(
    n, width, tok_ref, conv_ref, norm_ref, skip_ref, gain_ref, mi_ref, up_ref, down_ref, mo_ref,
    out_ref, resid, stats, first, regrouped, lowered, returned,
    st_send, st_recv, send_sem, recv_sem,
):
    me = lax.axis_index("chan")
    barrier = greet("chan", n)
    rows, cols = tok_ref.shape
    chunks, _, step = first.shape
    piece = rows // n
    skip, gain = column_of(skip_ref), column_of(gain_ref)

    def residual_of(c, carry):
        view = pl.ds(pl.multiple_of(c * step, step), step)
        value = (
            tok_ref[:, view].astype(jnp.float32)
            + conv_ref[:, view]
            + skip * norm_ref[:, view].astype(jnp.float32)
        ).astype(jnp.bfloat16)
        resid[:, view] = value
        value = value.astype(jnp.float32)
        stats[0, 0:1, view] = jnp.sum(value, axis=0, keepdims=True)
        stats[0, 1:2, view] = jnp.sum(value * value, axis=0, keepdims=True)
        return carry

    lax.fori_loop(0, chunks, residual_of, 0)
    pl.semaphore_wait(barrier, n - 1)
    total = share_stats(n, stats, st_send, st_recv)
    mean = total[0:1] / width
    stats[0, 0:1, :] = mean
    stats[0, 1:2, :] = lax.rsqrt(total[1:2] / width - mean * mean + 1e-05)

    def exchange(phase, c, k):
        peer = lax.rem(me + k, n)
        source, target = ((first, regrouped), (lowered, returned))[phase]
        return pltpu.make_async_remote_copy(
            src_ref=source.at[c, pl.ds(pl.multiple_of(peer * piece, 16), piece)],
            dst_ref=target.at[c, pl.ds(pl.multiple_of(me * piece, 16), piece)],
            send_sem=send_sem.at[phase, c, k],
            recv_sem=recv_sem.at[phase, c, k],
            device_id={"chan": peer},
            device_id_type=MESH,
        )

    own = pl.ds(pl.multiple_of(me * piece, 16), piece)

    def first_step(c, carry):
        view = pl.ds(pl.multiple_of(c * step, step), step)
        value = resid[:, view].astype(jnp.float32)
        value = (value - stats[0, 0:1, view]) * stats[0, 1:2, view] * gain
        first[c] = across(mi_ref[...], value.astype(jnp.bfloat16)).astype(jnp.bfloat16)
        for k in range(1, n):
            exchange(0, c, k).start()
        regrouped[c, own] = first[c, own]
        return carry

    lax.fori_loop(0, chunks, first_step, 0)

    def second_step(c, carry):
        for k in range(1, n):
            exchange(0, c, k).wait()
        pre = across(up_ref[...], regrouped[c])
        hidden = 0.5 * pre * (1.0 + lax.erf(pre * math.sqrt(0.5)))
        lowered[c] = across(down_ref[...], hidden.astype(jnp.bfloat16)).astype(jnp.bfloat16)
        for k in range(1, n):
            exchange(1, c, k).start()
        returned[c, own] = lowered[c, own]
        return carry

    lax.fori_loop(0, chunks, second_step, 0)

    def third_step(c, carry):
        view = pl.ds(pl.multiple_of(c * step, step), step)
        for k in range(1, n):
            exchange(1, c, k).wait()
        term = across(mo_ref[...], returned[c])
        out_ref[:, view] = (resid[:, view].astype(jnp.float32) + term).astype(jnp.bfloat16)
        return carry

    lax.fori_loop(0, chunks, third_step, 0)


def mlp(n, width, *operands):
    rows, cols = operands[0].shape
    step = 512 if cols % 512 == 0 else cols
    chunks = cols // step
    block = pltpu.VMEM((chunks, rows, step), jnp.bfloat16)
    dma = pltpu.SemaphoreType.DMA
    return pl.pallas_call(
        functools.partial(mlp_kernel, n, width),
        out_shape=jax.ShapeDtypeStruct((rows, cols), jnp.bfloat16),
        in_specs=[vmem_spec()] * len(operands),
        out_specs=vmem_spec(),
        scratch_shapes=[
            pltpu.VMEM((rows, cols), jnp.bfloat16),
            pltpu.VMEM((n, 2, cols), jnp.float32),
            block, block, block, block,
            dma((n,)), dma((n,)), dma((2, chunks, n)), dma((2, chunks, n)),
        ],
        compiler_params=pltpu.CompilerParams(
            collective_id=2, has_side_effects=True, vmem_limit_bytes=VMEM_BYTES
        ),
    )(*operands)


def shards(
    tokens,
    filter_spectrum,
    skip_weight,
    norm_gain,
    mlp_gain,
    mix_in,
    up_weight,
    down_weight,
    mix_out,
):
    columns, tok_rows = tokens.shape
    groups = lax.axis_size("seq")
    blocks = lax.axis_size("chan")
    width = columns * blocks
    hidden_width = up_weight.shape[1] // columns
    flats = (mix_in, up_weight, down_weight, mix_out)
    if groups == 8 and (tok_rows // groups) % 128 == 0:
        convolved, normed, *factors = convolve_kernel(
            groups, blocks, width, tokens, norm_gain, filter_spectrum, flats
        )
    else:
        normed = first_norm(blocks, width, tokens, norm_gain)
        cos_w, sin_w = dft_tables(RADIX)
        cos_a, sin_a = dft_tables(tok_rows // RADIX)
        cos_p, sin_p = dft_tables(groups)

        def swap(pair_in):
            return tuple(
                lax.all_to_all(half, "seq", split_axis=1, concat_axis=1, tiled=True)
                for half in pair_in
            )

        convolved = spectral(
            normed, filter_spectrum, (cos_w, sin_w, cos_a, sin_a), cos_p, sin_p, swap, swap
        )
        shapes = ((columns, columns), (columns, hidden_width), (hidden_width, columns))
        factors = [flat.reshape(shape) for flat, shape in zip(flats, shapes + shapes[:1])]
    return mlp(
        blocks,
        width,
        tokens,
        convolved,
        normed,
        skip_weight[None],
        mlp_gain[None],
        *factors,
    )


def solution(mesh):
    in_specs = (
        P("chan", "seq"),
        P(None, "chan", "seq"),
        P("chan"),
        P("chan"),
        P("chan"),
        P("chan", None),
        P("chan", None),
        P("chan", None),
        P("chan", None),
    )
    out_specs = P("chan", "seq")
    return jax.shard_map(shards, mesh=mesh, in_specs=in_specs, out_specs=out_specs, check_vma=False)
```
